256 devices in a mesh: len: 8 (over x, core), wid: 32 (over y, z).
Axes of the slice: x: 4, y: 4, z: 8, core: 2. Of those that a mesh axis runs over, the one named last changes fastest.
Arguments:
- velocity: float32 [2, 256, 1024, 256], P(None, 'len', 'wid'), may hold values from -6 to 6
- bfield: float32 [256, 1024, 256], P('len', 'wid'), may hold values from 0.5 to 1.5
- material: int32 [256, 1024, 256], P('len', 'wid'), may hold values from 0 to 2
- wall_mask: int32 [256, 1024, 256], P('len', 'wid'), may hold values 0 or 1
- potential_guess: float32 [256, 1024, 256], P('len', 'wid'), may hold values from -6 to 6
Outputs:
- new_velocity: float32 [2, 256, 1024, 256], P(None, 'len', 'wid')
- potential: float32 [256, 1024, 256], P('len', 'wid')
The draws below stay inside these ranges and needn't reach their ends.
All inputs are finite; a program needn't handle non-finite values. No bound on the sum of `wall_mask` on one device may be relied on, other than what follows from the above.
Results may differ from the reference program's by a relative error of at most 0.000026.
Values sent between devices are 32-bit elements; how exact they have to be, the bound alone decides.
A program may use at most 64 MiB of HBM per device.

```python
import jax
import jax.numpy as jnp

K = 256
SWEEPS = 4
NL = 256
NW = 1024


def plant(drawn, rng, least, top_value):
    dims = drawn.shape
    spot = [jax.random.randint(jax.random.fold_in(rng, axis), (), 0, dims[axis]) for axis in range(len(dims))]
    drawn = drawn.at[tuple(spot)].set(least)
    longest = dims.index(max(dims))
    spot[longest] = (spot[longest] + 1) % dims[longest]
    return drawn.at[tuple(spot)].set(top_value)


def steps_of(key, dims, split, low, high):
    loudness, own = 1.0, jax.random.fold_in(key, 6)
    for dim, shards_of in split:
        draws = jnp.exp(jax.random.uniform(jax.random.fold_in(own, dim), (shards_of,), jnp.float32, low / len(split), high / len(split)))
        loudness = loudness * jnp.repeat(draws, dims[dim] // shards_of).reshape([-1 if axis == dim else 1 for axis in range(len(dims))])
    return loudness


def scatter_about(rng, dims, spread, limit, shards=(), dtype=jnp.bfloat16):
    result = jax.random.normal(rng, dims, jnp.float32) * spread
    if len(shards) > 0:
        result = steps_of(rng, dims, shards, -0.22, 0.18) * result
    return jnp.clip(result, min=-limit, max=limit).astype(dtype)


def setup_inputs(seed: int = 0) -> dict:
    keys = jax.random.split(jax.random.key(seed), 6)
    velocity = scatter_about(keys[0], (2, NL, NW, K), 1.0, 6.0, ((1, 8), (2, 32)), jnp.float32)
    bfield = jnp.clip(0.5 + 1.0 * jax.random.uniform(keys[1], (NL, NW, K), jnp.float32) ** steps_of(keys[1], (NL, NW, K), ((0, 8), (1, 32)), -0.2, 0.2), 0.5, 1.5)
    material = plant(jax.random.randint(keys[2], (NL, NW, K), 0, 3), jax.random.fold_in(keys[2], 1), 0, 2).astype(jnp.int32)
    wall_mask = plant((jax.random.randint(keys[3], (NL, NW, K), 0, 4) < 1).astype(jnp.int32), jax.random.fold_in(keys[3], 1), 0, 1)
    potential_guess = scatter_about(keys[4], (NL, NW, K), 1.0, 6.0, ((0, 8), (1, 32)), jnp.float32)
    return dict(velocity=velocity, bfield=bfield, material=material, wall_mask=wall_mask, potential_guess=potential_guess)


CONTACT_GAIN = 2.0
TIME_STEP = 0.5
LOWER_BOUND = 0.1
UPPER_BOUND = 2.0
CENTRE_VALUE = 0.5 * (UPPER_BOUND + LOWER_BOUND)
HALF_SPREAD = 0.5 * (UPPER_BOUND - LOWER_BOUND)
RATIO_ONE = CENTRE_VALUE / HALF_SPREAD


def offset_view(field, i, j):
    rows = field.shape[0] - 2
    cols = field.shape[1] - 2
    return field[1 + i:1 + i + rows, 1 + j:1 + j + cols]


def upward(field):
    return jnp.concatenate([field[:, :, 1:], jnp.zeros_like(field[:, :, :1])], axis=2)


def downward(field):
    return jnp.concatenate([jnp.zeros_like(field[:, :, :1]), field[:, :, :-1]], axis=2)


def conductivity(material):
    melt = (material == 0).astype(jnp.float32)
    shell = (material == 1).astype(jnp.float32)
    copper = (material == 2).astype(jnp.float32)
    return 1.0 * melt + 0.5 * shell + 6.0 * copper


def operate(field, conduct, contact):
    centre = offset_view(field, 0, 0)
    own_cond = offset_view(conduct, 0, 0)
    summed = CONTACT_GAIN * contact * centre
    for i, j in ((1, 0), (-1, 0), (0, 1), (0, -1)):
        summed = summed + 0.5 * (own_cond + offset_view(conduct, i, j)) * (centre - offset_view(field, i, j))
    summed = summed + 0.5 * (own_cond + upward(own_cond)) * (centre - upward(centre))
    summed = summed + 0.5 * (own_cond + downward(own_cond)) * (centre - downward(centre))
    return summed


def diagonal_of(conduct, contact):
    own_cond = offset_view(conduct, 0, 0)
    summed = CONTACT_GAIN * contact
    for i, j in ((1, 0), (-1, 0), (0, 1), (0, -1)):
        summed = summed + 0.5 * (own_cond + offset_view(conduct, i, j))
    summed = summed + 0.5 * (own_cond + upward(own_cond))
    summed = summed + 0.5 * (own_cond + downward(own_cond))
    return summed


def source_of(conduct, field_len, field_wid):
    own_cond = offset_view(conduct, 0, 0)
    len_centre = offset_view(field_len, 0, 0)
    wid_centre = offset_view(field_wid, 0, 0)
    summed = -(0.5 * (own_cond + offset_view(conduct, 1, 0))) * (0.5 * (len_centre + offset_view(field_len, 1, 0)))
    summed = summed + (0.5 * (own_cond + offset_view(conduct, -1, 0))) * (0.5 * (len_centre + offset_view(field_len, -1, 0)))
    summed = summed - (0.5 * (own_cond + offset_view(conduct, 0, 1))) * (0.5 * (wid_centre + offset_view(field_wid, 0, 1)))
    summed = summed + (0.5 * (own_cond + offset_view(conduct, 0, -1))) * (0.5 * (wid_centre + offset_view(field_wid, 0, -1)))
    return summed


def padded(field):
    return jnp.pad(field, ((1, 1), (1, 1), (0, 0)))


def reference(velocity, bfield, material, wall_mask, potential_guess):
    conduct = conductivity(material)
    contact = wall_mask.astype(jnp.float32)
    field_len = velocity[1] * bfield
    field_wid = -velocity[0] * bfield
    cond_pad = padded(conduct)
    source = source_of(cond_pad, padded(field_len), padded(field_wid))
    diagonal = diagonal_of(cond_pad, contact)
    residual = source - operate(padded(potential_guess), cond_pad, contact)
    direction = residual / diagonal * (1.0 / CENTRE_VALUE)
    potential = potential_guess
    weight_now = 1.0 / RATIO_ONE
    for sweep in range(SWEEPS):
        potential = potential + direction
        if sweep < SWEEPS - 1:
            residual = residual - operate(padded(direction), cond_pad, contact)
            weight_next = 1.0 / (2.0 * RATIO_ONE - weight_now)
            keep_factor = weight_next * weight_now
            new_factor = 2.0 * weight_next / HALF_SPREAD
            direction = keep_factor * direction + new_factor * (residual / diagonal)
            weight_now = weight_next
    pot_pad = padded(potential)
    grad_len = 0.5 * (offset_view(pot_pad, 1, 0) - offset_view(pot_pad, -1, 0))
    grad_wid = 0.5 * (offset_view(pot_pad, 0, 1) - offset_view(pot_pad, 0, -1))
    current_len = conduct * (field_len - grad_len)
    current_wid = conduct * (field_wid - grad_wid)
    new_len = velocity[0] + TIME_STEP * current_wid * bfield
    new_wid = velocity[1] - TIME_STEP * current_len * bfield
    return jnp.stack([new_len, new_wid]), potential
```

```python
import functools

import jax
import jax.numpy as jnp
from jax import lax
from jax.experimental import pallas as pl
from jax.experimental.pallas import tpu as pltpu
from jax.sharding import PartitionSpec as P

MESH = pl.DeviceIdType.MESH
SWEEPS = 4
THETA = 0.5 * (2.0 + 0.1)
DELTA = 0.5 * (2.0 - 0.1)
S1 = THETA / DELTA

ROWS = 32
DEEP = 4
NAT0 = DEEP * 32
PAD = 8
TROWS = 64
TOWN = 16
TAREA = pl.ds(12, 40)
PW = 48
FIRST = (-4, 26)


def chebyshev():
    weight = 1.0 / S1
    gains, alphas, betas = [1.0 / THETA], [], []
    kf_old = nf_old = None
    for _ in range(SWEEPS - 1):
        weight_next = 1.0 / (2.0 * S1 - weight)
        kf, nf = weight_next * weight, 2.0 * weight_next / DELTA
        if nf_old is None:
            alphas.append(kf / nf + THETA - 1.0)
            betas.append(0.0)
        else:
            alphas.append(kf / nf + 1.0 / nf_old - 1.0)
            betas.append(-kf_old / (nf_old * nf_old))
        gains.append(nf * gains[-1])
        kf_old, nf_old, weight = kf, nf, weight_next
    return gains, alphas, betas


GAINS, ALPHAS, BETAS = chebyshev()


def lanes_of(shape):
    return lax.broadcasted_iota(jnp.int32, shape, 1)


def k_up(x, zero):
    r = [pltpu.roll(v, 127, 1) for v in x]
    last = lanes_of(x[0].shape) == 127
    return [jnp.where(last, r[1], r[0]), jnp.where(last, 0.0, r[1]) if zero else r[1]]


def k_down(x, zero):
    r = [pltpu.roll(v, 1, 1) for v in x]
    first = lanes_of(x[0].shape) == 0
    return [jnp.where(first, 0.0, r[0]) if zero else r[0], jnp.where(first, r[0], r[1])]


def kernel(n_len, n_wid, u_hbm, b_hbm, m_hbm, w_hbm, g_hbm, vel_out, pot_out,
           U0, U1, B, MAT, WALL, G, HL, HW, QP, QM, C, K, RP, DP, E0, E1, E2, E3, TN, GH,
           CT, KT, GT, QS, QR, E0T, E1T, E2T, E3T, TT, POT, lsem, ssem, rsem):
    li, wi = lax.axis_index("len"), lax.axis_index("wid")
    has = {(-1, 0): li > 0, (1, 0): li < n_len - 1, (0, -1): wi > 0, (0, 1): wi < n_wid - 1}
    for dl in (-1, 1):
        for dw in (-1, 1):
            has[dl, dw] = jnp.logical_and(has[dl, 0], has[0, dw])
    straight = ((0, -1), (0, 1), (-1, 0), (1, 0))
    diagonal = ((-1, -1), (-1, 1), (1, -1), (1, 1))

    barrier = pltpu.get_barrier_semaphore()
    for way in straight:
        @pl.when(has[way])
        def _():
            pl.semaphore_signal(barrier, inc=1, device_id=(li + way[0], wi + way[1]), device_id_type=MESH)

    own = pl.ds(PAD, 1024)
    loads = []
    for src, dst in (
        (m_hbm, lambda h: MAT.at[h]), (g_hbm, lambda h: G.at[h, own]), (b_hbm, lambda h: B.at[h]),
        (u_hbm.at[0], lambda h: U0.at[h]), (u_hbm.at[1], lambda h: U1.at[h]), (w_hbm, lambda h: WALL.at[h]),
    ):
        for h in range(2):
            copy = pltpu.make_async_copy(src.at[:, pl.ds(128 * h, 128)], dst(h), lsem.at[len(loads)])
            copy.start()
            loads.append(copy)

    for dl in (-1, 1):
        rows = pl.ds(0, 128) if dl < 0 else pl.ds(NAT0 + 1024, 128)
        @pl.when(jnp.logical_not(has[dl, 0]))
        def _():
            for ref in (C, K, E0, QP, QM):
                for h in range(2):
                    ref[h, rows, :] = jnp.zeros((128, 128), jnp.float32)
            for h in range(2):
                GH[(dl + 1) // 2, h] = jnp.zeros((32, 128), jnp.float32)
    for dw in (-1, 1):
        side = (dw + 1) // 2
        c0 = 0 if dw < 0 else 6
        @pl.when(jnp.logical_not(has[0, dw]))
        def _():
            for h in range(2):
                QR[side, h] = jnp.zeros((32, 128), jnp.float32)
                for c in range(c0, c0 + 4):
                    for ref in (CT, KT, GT, E0T):
                        ref[side, c, h, pl.ds(TOWN, 32), :] = jnp.zeros((32, 128), jnp.float32)
    for dl, dw in diagonal:
        side = (dw + 1) // 2
        c0 = 0 if dw < 0 else 6
        @pl.when(jnp.logical_not(has[dl, dw]))
        def _():
            for h in range(2):
                for c in range(c0, c0 + 4):
                    for ref in (CT, KT, E0T):
                        ref[side, c, h, pl.ds(8 if dl < 0 else 48, 8), :] = jnp.zeros((8, 128), jnp.float32)

    for copy in loads:
        copy.wait()

    def prepare(i, carry):
        n = pl.multiple_of(32 * i, 32)
        o, p = pl.multiple_of(NAT0 + n, 32), pl.multiple_of(PAD + n, 8)
        for h in range(2):
            m = MAT[h, pl.ds(n, 32), :]
            b, g = B[h, pl.ds(n, 32), :], G[h, pl.ds(p, 32), :]
            hl = 0.5 * (U1[h, pl.ds(n, 32), :] * b)
            C[h, pl.ds(o, 32), :] = jnp.where(m == 0, 1.0, jnp.where(m == 1, 0.5, 6.0))
            K[h, pl.ds(o, 32), :] = WALL[h, pl.ds(n, 32), :].astype(jnp.float32)
            HL[h, pl.ds(n, 32), :] = hl
            HW[h, pl.ds(p, 32), :] = -0.5 * (U0[h, pl.ds(n, 32), :] * b)
            QP[h, pl.ds(o, 32), :] = g + hl
            QM[h, pl.ds(o, 32), :] = g - hl
        return carry

    lax.fori_loop(0, 32, prepare, 0)

    def column(ref, h, first, col, rows=32):
        return ref[h, pl.ds(first + col, rows, stride=32), :]

    own_t = pl.ds(TOWN, 32)
    for side in range(2):
        for col in range(0, 6) if side == 0 else range(26, 32):
            c = col - FIRST[side]
            for h in range(2):
                CT[side, c, h, own_t, :] = column(C, h, NAT0, col)
                KT[side, c, h, own_t, :] = column(K, h, NAT0, col)
                if 3 <= c <= 6:
                    GT[side, c, h, own_t, :] = column(G, h, PAD, col)
    for h in range(2):
        QS[0, h] = GT[0, 4, h, own_t, :] - column(HW, h, PAD, 0)
        QS[1, h] = GT[1, 5, h, own_t, :] + column(HW, h, PAD, 31)

    sent = []

    def message(way, src, dst):
        k = len(sent)
        copy = pltpu.make_async_remote_copy(
            src, dst, ssem.at[k], rsem.at[k], device_id=(li + way[0], wi + way[1]), device_id_type=MESH
        )
        sent.append((way, copy))
        @pl.when(has[way])
        def _():
            copy.start()
        return way, copy

    def received(messages):
        for way, copy in messages:
            @pl.when(has[-way[0], -way[1]])
            def _():
                copy.wait_recv()

    def nat_part(ref, way, depth, here):
        if way[0] < 0:
            first = NAT0 if here else NAT0 + 1024
        else:
            first = NAT0 + 1024 - 32 * depth if here else NAT0 - 32 * depth
        return ref.at[:, pl.ds(first, 32 * depth), :]

    def strip_part(ref, way, near, far, here):
        count = far - near + 1
        if way[1] < 0:
            side, first = (0, 3 + near) if here else (1, 5 + near)
        else:
            side, first = (1, 6 - far) if here else (0, 4 - far)
        if way[0] == 0:
            rows = own_t
        elif way[0] < 0:
            rows = pl.ds(16 if here else 48, 8)
        else:
            rows = pl.ds(40 if here else 8, 8)
        return ref.at[side, pl.ds(first, count), :, rows, :]

    pl.semaphore_wait(barrier, sum(has[way].astype(jnp.int32) for way in straight))

    wid_ways, len_ways = straight[:2], straight[2:]
    first_wid, first_len, later_len, later_wid = [], [], [], []
    for way in wid_ways:
        out, into = (0, 1) if way[1] < 0 else (1, 0)
        first_wid.append(message(way, QS.at[out], QR.at[into]))
        first_wid.append(message(way, strip_part(CT, way, 1, 1, True), strip_part(CT, way, 1, 1, False)))
    for way in len_ways:
        Q = QM if way[0] < 0 else QP
        first_len.append(message(way, nat_part(Q, way, 1, True), nat_part(Q, way, 1, False)))
        first_len.append(message(way, nat_part(C, way, 4, True), nat_part(C, way, 4, False)))
    for way in wid_ways:
        later_wid.append(message(way, strip_part(CT, way, 2, 4, True), strip_part(CT, way, 2, 4, False)))
        later_wid.append(message(way, strip_part(KT, way, 1, 3, True), strip_part(KT, way, 1, 3, False)))
        later_wid.append(message(way, strip_part(GT, way, 1, 1, True), strip_part(GT, way, 1, 1, False)))
    for way in len_ways:
        into = 1 if way[0] < 0 else 0
        first = PAD if way[0] < 0 else PAD + 31 * 32
        later_len.append(message(way, nat_part(K, way, 3, True), nat_part(K, way, 3, False)))
        later_len.append(message(way, G.at[:, pl.ds(first, 32), :], GH.at[into]))

    shape = (32, 128)
    jj = lax.broadcasted_iota(jnp.int32, shape, 0)
    lane = lanes_of(shape)

    def put_coefficients(iv, h, s, store):
        for q in range(6):
            t = s[q] * iv
            if q == 4 and h == 0:
                t = jnp.where(lanes_of(t.shape) == 0, 0.0, t)
            if q == 5 and h == 1:
                t = jnp.where(lanes_of(t.shape) == 127, 0.0, t)
            store(q, t)

    def row(i, valid=None):
        n = pl.multiple_of(32 * i, 32)
        o = pl.multiple_of(NAT0 + n, 32)
        p = pl.multiple_of(PAD + n, 8)
        c = [C[h, pl.ds(o, 32), :] for h in range(2)]
        cu, cd = k_up(c, True), k_down(c, True)
        if valid is None:
            g = [G[h, pl.ds(p, 32), :] for h in range(2)]
            gu, gd = k_up(g, True), k_down(g, True)
        for h in range(2):
            slm = 0.5 * (c[h] + C[h, pl.ds(o - 32, 32), :])
            slp = 0.5 * (c[h] + C[h, pl.ds(o + 32, 32), :])
            swm = jnp.where(jj == 0, 0.0, 0.5 * (c[h] + C[h, pl.ds(o - 1, 32), :]))
            swp = jnp.where(jj == 31, 0.0, 0.5 * (c[h] + C[h, pl.ds(o + 1, 32), :]))
            skm, skp = 0.5 * (c[h] + cd[h]), 0.5 * (c[h] + cu[h])
            k2 = 2.0 * K[h, pl.ds(o, 32), :]
            diag = k2 + ((slm + slp) + (swm + swp)) + (skm + skp)
            iv = 1.0 / diag
            if valid is None:
                hl, hw = HL[h, pl.ds(n, 32), :], HW[h, pl.ds(p, 32), :]
                gwm = jnp.where(jj == 0, 0.0, G[h, pl.ds(p - 1, 32), :] + HW[h, pl.ds(p - 1, 32), :] + hw)
                gwp = jnp.where(jj == 31, 0.0, G[h, pl.ds(p + 1, 32), :] - HW[h, pl.ds(p + 1, 32), :] - hw)
                res = slm * (QP[h, pl.ds(o - 32, 32), :] + hl) + slp * (QM[h, pl.ds(o + 32, 32), :] - hl)
                res = res + (swm * gwm + swp * gwp) + (skm * gd[h] + skp * gu[h]) - diag * g[h]
                RP[h, pl.ds(n, 32), :] = res
                DP[h, pl.ds(n, 32), :] = diag
                E0[h, pl.ds(o, 32), :] = res * iv
            else:
                iv = jnp.where(valid, iv, 0.0)

            def store(q, t):
                TN[q, h, pl.ds(o, 32), :] = t

            put_coefficients(iv, h, (slm, slp, swm, swp, skm, skp), store)

    def row_step(i, carry):
        row(i)
        return carry

    lax.fori_loop(1, 31, row_step, 0)

    received(first_len)
    row(0)
    row(31)
    later_diag = []
    for way in diagonal:
        later_diag.append(message(way, strip_part(CT, way, 1, 4, True), strip_part(CT, way, 1, 4, False)))
        later_diag.append(message(way, strip_part(KT, way, 1, 4, True), strip_part(KT, way, 1, 4, False)))

    received(first_wid)
    for side, col, halo, sign in ((0, 0, 3, 1.0), (1, 31, 6, -1.0)):
        for h in range(2):
            c = CT[side, col - FIRST[side], h, own_t, :]
            s = 0.5 * (c + CT[side, halo, h, own_t, :])
            res = column(RP, h, 0, col) + s * (
                QR[side, h] + sign * column(HW, h, PAD, col) - column(G, h, PAD, col)
            )
            e = res / (column(DP, h, 0, col) + s)
            E0T[side, col - FIRST[side], h, own_t, :] = e
            E0[h, pl.ds(NAT0 + col, 32, stride=32), :] = e
    for side in range(2):
        for col in range(1, 4) if side == 0 else range(28, 31):
            for h in range(2):
                E0T[side, col - FIRST[side], h, own_t, :] = column(E0, h, NAT0, col)

    second = []
    for way in wid_ways:
        second.append(message(way, strip_part(E0T, way, 1, 4, True), strip_part(E0T, way, 1, 4, False)))
    for way in diagonal:
        second.append(message(way, strip_part(E0T, way, 1, 4, True), strip_part(E0T, way, 1, 4, False)))
    for way in len_ways:
        second.append(message(way, nat_part(E0, way, 4, True), nat_part(E0, way, 4, False)))

    for side in range(2):
        for col in range(4, 6) if side == 0 else range(26, 28):
            for h in range(2):
                E0T[side, col - FIRST[side], h, own_t, :] = column(E0, h, NAT0, col)

    E = (E0, E1, E2, E3)
    ET = (E0T, E1T, E2T, E3T)

    def sweep_row(k, r):
        o = pl.multiple_of(32 * r, 32)
        src = E[k]
        x = [src[h, pl.ds(o, 32), :] for h in range(2)]
        xu, xd = k_up(x, False), k_down(x, False)
        for h in range(2):
            def t(q):
                return TN[q, h, pl.ds(o, 32), :]
            total = ALPHAS[k] * x[h] + t(4) * xd[h] + t(5) * xu[h]
            total = total + t(0) * src[h, pl.ds(o - 32, 32), :] + t(1) * src[h, pl.ds(o + 32, 32), :]
            total = total + t(2) * src[h, pl.ds(o - 1, 32), :] + t(3) * src[h, pl.ds(o + 1, 32), :]
            if k > 0:
                total = total + BETAS[k] * E[k - 1][h, pl.ds(o, 32), :]
            E[k + 1][h, pl.ds(o, 32), :] = total

    def sweep(k, first, last):
        def step(r, carry):
            sweep_row(k, r)
            return carry
        lax.fori_loop(first + DEEP, last + 1 + DEEP, step, 0)

    def potential_row(i, guess):
        o = pl.multiple_of(NAT0 + 32 * i, 32)
        q = pl.multiple_of(PW * (i + DEEP) + 8, 8)
        for h in range(2):
            total = guess(h)
            for k in range(SWEEPS):
                total = total + GAINS[k] * E[k][h, pl.ds(o, 32), :]
            POT[h, pl.ds(q, 32), :] = total

    def own_potential(first, last):
        def step(i, carry):
            p = pl.multiple_of(PAD + 32 * i, 8)
            potential_row(i, lambda h: G[h, pl.ds(p, 32), :])
            return carry
        lax.fori_loop(first, last + 1, step, 0)

    sweep(0, 1, 30)
    sweep(1, 2, 29)
    sweep(2, 3, 28)
    own_potential(3, 28)

    def force(i, carry):
        n = pl.multiple_of(32 * i, 32)
        o, p = pl.multiple_of(NAT0 + n, 32), pl.multiple_of(PAD + n, 8)
        for h in range(2):
            at = (h, pl.ds(n, 32), slice(None))
            cb = C[h, pl.ds(o, 32), :] * B[at]
            U0[at] = U0[at] + cb * HW[h, pl.ds(p, 32), :]
            U1[at] = U1[at] - cb * HL[at]
            B[at] = 0.25 * cb
        return carry

    lax.fori_loop(0, 32, force, 0)

    received(later_len)
    received(later_wid)
    received(later_diag)
    for i in (-3, -2, -1):
        row(i, has[-1, 0])
        row(31 - i, has[1, 0])
    for side in range(2):
        for col in range(0, 6) if side == 0 else range(26, 32):
            c = col - FIRST[side]
            for h in range(2):
                CT[side, c, h, pl.ds(12, 4), :] = column(C, h, 0, col, 4)
                CT[side, c, h, pl.ds(48, 4), :] = column(C, h, NAT0 + 1024, col, 4)
                KT[side, c, h, pl.ds(13, 3), :] = column(K, h, 32, col, 3)
                KT[side, c, h, pl.ds(48, 3), :] = column(K, h, NAT0 + 1024, col, 3)

    ii = lax.broadcasted_iota(jnp.int32, (40, 128), 0)
    rows_in = jnp.logical_and(
        jnp.logical_or(ii >= 4, has[-1, 0]), jnp.logical_or(ii < 36, has[1, 0])
    )

    for side in range(2):
        has_side = has[0, -1 if side == 0 else 1]

        def strip(c, carry):
            x = [CT[side, c, h, TAREA, :] for h in range(2)]
            cu, cd = k_up(x, True), k_down(x, True)
            in_own = c >= 4 if side == 0 else c < 6
            valid = jnp.logical_and(rows_in, jnp.logical_or(in_own, has_side))
            for h in range(2):
                slm = 0.5 * (x[h] + CT[side, c, h, pl.ds(11, 40), :])
                slp = 0.5 * (x[h] + CT[side, c, h, pl.ds(13, 40), :])
                swm = 0.5 * (x[h] + CT[side, c - 1, h, TAREA, :])
                swp = 0.5 * (x[h] + CT[side, c + 1, h, TAREA, :])
                skm, skp = 0.5 * (x[h] + cd[h]), 0.5 * (x[h] + cu[h])
                diag = 2.0 * KT[side, c, h, TAREA, :] + ((slm + slp) + (swm + swp)) + (skm + skp)
                iv = jnp.where(valid, 1.0 / diag, 0.0)

                def store(q, t):
                    TT[q, side, c, h, TAREA, :] = t

                put_coefficients(iv, h, (slm, slp, swm, swp, skm, skp), store)
            return carry

        lax.fori_loop(1, 9, strip, 0)

    received(second)

    for side in range(2):
        for col in range(0, 6) if side == 0 else range(26, 32):
            c = col - FIRST[side]
            for h in range(2):
                E0T[side, c, h, pl.ds(12, 4), :] = column(E0, h, 0, col, 4)
                E0T[side, c, h, pl.ds(48, 4), :] = column(E0, h, NAT0 + 1024, col, 4)

    for k in range(SWEEPS - 1):
        for side in range(2):
            def strip_sweep(c, carry):
                src = ET[k]
                x = [src[side, c, h, TAREA, :] for h in range(2)]
                xu, xd = k_up(x, False), k_down(x, False)
                for h in range(2):
                    def t(q):
                        return TT[q, side, c, h, TAREA, :]
                    total = ALPHAS[k] * x[h] + t(4) * xd[h] + t(5) * xu[h]
                    total = total + t(0) * src[side, c, h, pl.ds(11, 40), :] + t(1) * src[side, c, h, pl.ds(13, 40), :]
                    total = total + t(2) * src[side, c - 1, h, TAREA, :] + t(3) * src[side, c + 1, h, TAREA, :]
                    if k > 0:
                        total = total + BETAS[k] * ET[k - 1][side, c, h, TAREA, :]
                    ET[k + 1][side, c, h, TAREA, :] = total
                return carry

            lax.fori_loop(1 + k, 9 - k, strip_sweep, 0)
        sweep(k, k - 3, k)
        sweep(k, 31 - k, 34 - k)

    own_potential(0, 2)
    own_potential(29, 31)
    potential_row(-1, lambda h: GH[0, h])
    potential_row(32, lambda h: GH[1, h])
    for side in range(2):
        for c in range(3, 7):
            col = c + FIRST[side]
            for h in range(2):
                if 0 <= col < 32:
                    GT[side, c, h, pl.ds(15, 1), :] = GH[0, h, pl.ds(col, 1), :]
                    GT[side, c, h, pl.ds(48, 1), :] = GH[1, h, pl.ds(col, 1), :]
                total = GT[side, c, h, TAREA, :]
                for k in range(SWEEPS):
                    total = total + GAINS[k] * ET[k][side, c, h, TAREA, :]
                POT[h, pl.ds(8 + col, 40, stride=PW), :] = total

    def finish(i, carry):
        n = pl.multiple_of(32 * i, 32)
        q = pl.multiple_of(PW * (i + DEEP) + 8, 8)
        for h in range(2):
            at = (h, pl.ds(n, 32), slice(None))
            lanes = pl.ds(128 * h, 128)
            pot_out[pl.ds(n, 32), lanes] = POT[h, pl.ds(q, 32), :]
            vel_out[0, pl.ds(n, 32), lanes] = U0[at] - B[at] * (
                POT[h, pl.ds(q + 1, 32), :] - POT[h, pl.ds(q - 1, 32), :]
            )
            vel_out[1, pl.ds(n, 32), lanes] = U1[at] + B[at] * (
                POT[h, pl.ds(q + PW, 32), :] - POT[h, pl.ds(q - PW, 32), :]
            )
        return carry

    lax.fori_loop(0, 32, finish, 0)

    for way, copy in sent:
        @pl.when(has[way])
        def _():
            copy.wait_send()


N_MESSAGES = 34


def solution(mesh):
    n_len, n_wid = mesh.shape["len"], mesh.shape["wid"]

    def body(velocity, bfield, material, wall_mask, potential_guess):
        flat = lambda a: a.reshape(a.shape[:-3] + (1024, 256))
        own = pltpu.VMEM((2, 1024, 128), jnp.float32)
        padded = pltpu.VMEM((2, 1024 + 2 * PAD, 128), jnp.float32)
        nat = pltpu.VMEM((2, 1024 + 2 * NAT0, 128), jnp.float32)
        strip = pltpu.VMEM((2, 10, 2, TROWS, 128), jnp.float32)
        ints = pltpu.VMEM((2, 1024, 128), jnp.int32)
        rows = pltpu.VMEM((2, 2, 32, 128), jnp.float32)
        scratch = [
            own, own, own, ints, ints, padded, own, padded, nat, nat, nat, nat, own, own, nat, nat, nat, nat,
            pltpu.VMEM((6, 2, 1024 + 2 * NAT0, 128), jnp.float32), rows,
            strip, strip, strip, rows, rows, strip, strip, strip, strip,
            pltpu.VMEM((6, 2, 10, 2, TROWS, 128), jnp.float32),
            pltpu.VMEM((2, 40 * PW, 128), jnp.float32),
            pltpu.SemaphoreType.DMA((12,)),
            pltpu.SemaphoreType.DMA((N_MESSAGES,)),
            pltpu.SemaphoreType.DMA((N_MESSAGES,)),
        ]
        vel, pot = pl.pallas_call(
            functools.partial(kernel, n_len, n_wid),
            out_shape=(
                jax.ShapeDtypeStruct((2, 1024, 256), jnp.float32),
                jax.ShapeDtypeStruct((1024, 256), jnp.float32),
            ),
            in_specs=[pl.BlockSpec(memory_space=pltpu.HBM)] * 5,
            out_specs=(pl.BlockSpec(memory_space=pltpu.VMEM), pl.BlockSpec(memory_space=pltpu.VMEM)),
            scratch_shapes=scratch,
            compiler_params=pltpu.CompilerParams(
                collective_id=0, has_side_effects=True, vmem_limit_bytes=58 * 1024 * 1024
            ),
        )(flat(velocity), flat(bfield), flat(material), flat(wall_mask), flat(potential_guess))
        return vel.reshape(velocity.shape), pot.reshape(bfield.shape)

    whole, part = P(None, "len", "wid", None), P("len", "wid", None)
    return jax.shard_map(
        body,
        mesh=mesh,
        in_specs=(whole, part, part, part, part),
        out_specs=(whole, part),
        check_vma=False,
    )
```

```python
import functools

import jax
import jax.numpy as jnp
from jax import lax
from jax.experimental import pallas as pl
from jax.experimental.pallas import tpu as pltpu
from jax.sharding import PartitionSpec as P

MESH = pl.DeviceIdType.MESH
SWEEPS = 4
THETA = 0.5 * (2.0 + 0.1)
DELTA = 0.5 * (2.0 - 0.1)
S1 = THETA / DELTA

ROWS = 32
DEEP = 4
NAT0 = DEEP * 32
PAD = 8
TROWS = 64
TOWN = 16
TAREA = pl.ds(12, 40)
PW = 48
FIRST = (-4, 26)


def chebyshev():
    weight = 1.0 / S1
    gains, alphas, betas = [1.0 / THETA], [], []
    kf_old = nf_old = None
    for _ in range(SWEEPS - 1):
        weight_next = 1.0 / (2.0 * S1 - weight)
        kf, nf = weight_next * weight, 2.0 * weight_next / DELTA
        if nf_old is None:
            alphas.append(kf / nf + THETA - 1.0)
            betas.append(0.0)
        else:
            alphas.append(kf / nf + 1.0 / nf_old - 1.0)
            betas.append(-kf_old / (nf_old * nf_old))
        gains.append(nf * gains[-1])
        kf_old, nf_old, weight = kf, nf, weight_next
    return gains, alphas, betas


GAINS, ALPHAS, BETAS = chebyshev()


def lanes_of(shape):
    return lax.broadcasted_iota(jnp.int32, shape, 1)


def k_up(x, zero):
    r = [pltpu.roll(v, 127, 1) for v in x]
    last = lanes_of(x[0].shape) == 127
    return [jnp.where(last, r[1], r[0]), jnp.where(last, 0.0, r[1]) if zero else r[1]]


def k_down(x, zero):
    r = [pltpu.roll(v, 1, 1) for v in x]
    first = lanes_of(x[0].shape) == 0
    return [jnp.where(first, 0.0, r[0]) if zero else r[0], jnp.where(first, r[0], r[1])]


def kernel(n_len, n_wid, u_hbm, b_hbm, m_hbm, w_hbm, g_hbm, vel_out, pot_out,
           U0, U1, B, MAT, WALL, G, HL, HW, QP, QM, C, K, RP, DP, E0, E1, E2, E3, TN, GH,
           CT, KT, GT, QS, QR, E0T, E1T, E2T, E3T, TT, POT, lsem, ssem, rsem):
    li, wi = lax.axis_index("len"), lax.axis_index("wid")
    has = {(-1, 0): li > 0, (1, 0): li < n_len - 1, (0, -1): wi > 0, (0, 1): wi < n_wid - 1}
    for dl in (-1, 1):
        for dw in (-1, 1):
            has[dl, dw] = jnp.logical_and(has[dl, 0], has[0, dw])
    straight = ((0, -1), (0, 1), (-1, 0), (1, 0))
    diagonal = ((-1, -1), (-1, 1), (1, -1), (1, 1))

    barrier = pltpu.get_barrier_semaphore()
    for way in straight:
        @pl.when(has[way])
        def _():
            pl.semaphore_signal(barrier, inc=1, device_id=(li + way[0], wi + way[1]), device_id_type=MESH)

    own = pl.ds(PAD, 1024)
    loads = []
    for src, dst in (
        (m_hbm, lambda h: MAT.at[h]), (g_hbm, lambda h: G.at[h, own]), (b_hbm, lambda h: B.at[h]),
        (u_hbm.at[0], lambda h: U0.at[h]), (u_hbm.at[1], lambda h: U1.at[h]), (w_hbm, lambda h: WALL.at[h]),
    ):
        for h in range(2):
            copy = pltpu.make_async_copy(src.at[:, pl.ds(128 * h, 128)], dst(h), lsem.at[len(loads)])
            copy.start()
            loads.append(copy)

    for dl in (-1, 1):
        rows = pl.ds(0, 128) if dl < 0 else pl.ds(NAT0 + 1024, 128)
        @pl.when(jnp.logical_not(has[dl, 0]))
        def _():
            for ref in (C, K, E0, QP, QM):
                for h in range(2):
                    ref[h, rows, :] = jnp.zeros((128, 128), jnp.float32)
            for h in range(2):
                GH[(dl + 1) // 2, h] = jnp.zeros((32, 128), jnp.float32)
    for dw in (-1, 1):
        side = (dw + 1) // 2
        c0 = 0 if dw < 0 else 6
        @pl.when(jnp.logical_not(has[0, dw]))
        def _():
            for h in range(2):
                QR[side, h] = jnp.zeros((32, 128), jnp.float32)
                for c in range(c0, c0 + 4):
                    for ref in (CT, KT, GT, E0T):
                        ref[side, c, h, pl.ds(TOWN, 32), :] = jnp.zeros((32, 128), jnp.float32)
    for dl, dw in diagonal:
        side = (dw + 1) // 2
        c0 = 0 if dw < 0 else 6
        @pl.when(jnp.logical_not(has[dl, dw]))
        def _():
            for h in range(2):
                for c in range(c0, c0 + 4):
                    for ref in (CT, KT, E0T):
                        ref[side, c, h, pl.ds(8 if dl < 0 else 48, 8), :] = jnp.zeros((8, 128), jnp.float32)

    for copy in loads:
        copy.wait()

    def prepare(i, carry):
        n = pl.multiple_of(32 * i, 32)
        o, p = pl.multiple_of(NAT0 + n, 32), pl.multiple_of(PAD + n, 8)
        for h in range(2):
            m = MAT[h, pl.ds(n, 32), :]
            b, g = B[h, pl.ds(n, 32), :], G[h, pl.ds(p, 32), :]
            hl = 0.5 * (U1[h, pl.ds(n, 32), :] * b)
            C[h, pl.ds(o, 32), :] = jnp.where(m == 0, 1.0, jnp.where(m == 1, 0.5, 6.0))
            K[h, pl.ds(o, 32), :] = WALL[h, pl.ds(n, 32), :].astype(jnp.float32)
            HL[h, pl.ds(n, 32), :] = hl
            HW[h, pl.ds(p, 32), :] = -0.5 * (U0[h, pl.ds(n, 32), :] * b)
            QP[h, pl.ds(o, 32), :] = g + hl
            QM[h, pl.ds(o, 32), :] = g - hl
        return carry

    lax.fori_loop(0, 32, prepare, 0, unroll=2)

    def column(ref, h, first, col, rows=32):
        return ref[h, pl.ds(first + col, rows, stride=32), :]

    own_t = pl.ds(TOWN, 32)
    for side in range(2):
        for col in range(0, 6) if side == 0 else range(26, 32):
            c = col - FIRST[side]
            for h in range(2):
                CT[side, c, h, own_t, :] = column(C, h, NAT0, col)
                KT[side, c, h, own_t, :] = column(K, h, NAT0, col)
                if 3 <= c <= 6:
                    GT[side, c, h, own_t, :] = column(G, h, PAD, col)
    for h in range(2):
        QS[0, h] = GT[0, 4, h, own_t, :] - column(HW, h, PAD, 0)
        QS[1, h] = GT[1, 5, h, own_t, :] + column(HW, h, PAD, 31)

    sent = []

    def message(way, src, dst):
        k = len(sent)
        copy = pltpu.make_async_remote_copy(
            src, dst, ssem.at[k], rsem.at[k], device_id=(li + way[0], wi + way[1]), device_id_type=MESH
        )
        sent.append((way, copy))
        @pl.when(has[way])
        def _():
            copy.start()
        return way, copy

    def received(messages):
        for way, copy in messages:
            @pl.when(has[-way[0], -way[1]])
            def _():
                copy.wait_recv()

    def nat_part(ref, way, depth, here):
        if way[0] < 0:
            first = NAT0 if here else NAT0 + 1024
        else:
            first = NAT0 + 1024 - 32 * depth if here else NAT0 - 32 * depth
        return ref.at[:, pl.ds(first, 32 * depth), :]

    def strip_part(ref, way, near, far, here):
        count = far - near + 1
        if way[1] < 0:
            side, first = (0, 3 + near) if here else (1, 5 + near)
        else:
            side, first = (1, 6 - far) if here else (0, 4 - far)
        if way[0] == 0:
            rows = own_t
        elif way[0] < 0:
            rows = pl.ds(16 if here else 48, 4)
        else:
            rows = pl.ds(44 if here else 12, 4)
        return ref.at[side, pl.ds(first, count), :, rows, :]

    pl.semaphore_wait(barrier, sum(has[way].astype(jnp.int32) for way in straight))

    wid_ways, len_ways = straight[:2], straight[2:]
    first_wid, first_len, later_len, later_wid = [], [], [], []
    for way in wid_ways:
        out, into = (0, 1) if way[1] < 0 else (1, 0)
        first_wid.append(message(way, QS.at[out], QR.at[into]))
        first_wid.append(message(way, strip_part(CT, way, 1, 1, True), strip_part(CT, way, 1, 1, False)))
    for way in len_ways:
        Q = QM if way[0] < 0 else QP
        first_len.append(message(way, nat_part(Q, way, 1, True), nat_part(Q, way, 1, False)))
        first_len.append(message(way, nat_part(C, way, 4, True), nat_part(C, way, 4, False)))
    for way in wid_ways:
        later_wid.append(message(way, strip_part(CT, way, 2, 4, True), strip_part(CT, way, 2, 4, False)))
        later_wid.append(message(way, strip_part(KT, way, 1, 3, True), strip_part(KT, way, 1, 3, False)))
        later_wid.append(message(way, strip_part(GT, way, 1, 1, True), strip_part(GT, way, 1, 1, False)))
    for way in len_ways:
        into = 1 if way[0] < 0 else 0
        first = PAD if way[0] < 0 else PAD + 31 * 32
        later_len.append(message(way, nat_part(K, way, 3, True), nat_part(K, way, 3, False)))
        later_len.append(message(way, G.at[:, pl.ds(first, 32), :], GH.at[into]))

    shape = (32, 128)
    jj = lax.broadcasted_iota(jnp.int32, shape, 0)
    lane = lanes_of(shape)

    def put_coefficients(iv, h, s, store):
        for q in range(6):
            t = s[q] * iv
            if q == 4 and h == 0:
                t = jnp.where(lanes_of(t.shape) == 0, 0.0, t)
            if q == 5 and h == 1:
                t = jnp.where(lanes_of(t.shape) == 127, 0.0, t)
            store(q, t)

    def row(i, valid=None):
        n = pl.multiple_of(32 * i, 32)
        o = pl.multiple_of(NAT0 + n, 32)
        p = pl.multiple_of(PAD + n, 8)
        c = [C[h, pl.ds(o, 32), :] for h in range(2)]
        cu, cd = k_up(c, True), k_down(c, True)
        if valid is None:
            g = [G[h, pl.ds(p, 32), :] for h in range(2)]
            gu, gd = k_up(g, True), k_down(g, True)
        for h in range(2):
            slm = 0.5 * (c[h] + C[h, pl.ds(o - 32, 32), :])
            slp = 0.5 * (c[h] + C[h, pl.ds(o + 32, 32), :])
            swm = jnp.where(jj == 0, 0.0, 0.5 * (c[h] + C[h, pl.ds(o - 1, 32), :]))
            swp = jnp.where(jj == 31, 0.0, 0.5 * (c[h] + C[h, pl.ds(o + 1, 32), :]))
            skm, skp = 0.5 * (c[h] + cd[h]), 0.5 * (c[h] + cu[h])
            k2 = 2.0 * K[h, pl.ds(o, 32), :]
            diag = k2 + ((slm + slp) + (swm + swp)) + (skm + skp)
            iv = 1.0 / diag
            if valid is None:
                hl, hw = HL[h, pl.ds(n, 32), :], HW[h, pl.ds(p, 32), :]
                gwm = jnp.where(jj == 0, 0.0, G[h, pl.ds(p - 1, 32), :] + HW[h, pl.ds(p - 1, 32), :] + hw)
                gwp = jnp.where(jj == 31, 0.0, G[h, pl.ds(p + 1, 32), :] - HW[h, pl.ds(p + 1, 32), :] - hw)
                res = slm * (QP[h, pl.ds(o - 32, 32), :] + hl) + slp * (QM[h, pl.ds(o + 32, 32), :] - hl)
                res = res + (swm * gwm + swp * gwp) + (skm * gd[h] + skp * gu[h]) - diag * g[h]
                RP[h, pl.ds(n, 32), :] = res
                DP[h, pl.ds(n, 32), :] = diag
                E0[h, pl.ds(o, 32), :] = res * iv
            else:
                iv = jnp.where(valid, iv, 0.0)

            def store(q, t):
                TN[q, h, pl.ds(o, 32), :] = t

            put_coefficients(iv, h, (slm, slp, swm, swp, skm, skp), store)

    def row_step(i, carry):
        row(i)
        return carry

    lax.fori_loop(1, 31, row_step, 0, unroll=2)

    received(first_len)
    row(0)
    row(31)
    later_diag = []
    for way in diagonal:
        later_diag.append(message(way, strip_part(CT, way, 1, 3, True), strip_part(CT, way, 1, 3, False)))
        later_diag.append(message(way, strip_part(KT, way, 1, 2, True), strip_part(KT, way, 1, 2, False)))

    received(first_wid)
    for side, col, halo, sign in ((0, 0, 3, 1.0), (1, 31, 6, -1.0)):
        for h in range(2):
            c = CT[side, col - FIRST[side], h, own_t, :]
            s = 0.5 * (c + CT[side, halo, h, own_t, :])
            res = column(RP, h, 0, col) + s * (
                QR[side, h] + sign * column(HW, h, PAD, col) - column(G, h, PAD, col)
            )
            e = res / (column(DP, h, 0, col) + s)
            E0T[side, col - FIRST[side], h, own_t, :] = e
            E0[h, pl.ds(NAT0 + col, 32, stride=32), :] = e
    for side in range(2):
        for col in range(1, 4) if side == 0 else range(28, 31):
            for h in range(2):
                E0T[side, col - FIRST[side], h, own_t, :] = column(E0, h, NAT0, col)

    second = []
    for way in wid_ways:
        second.append(message(way, strip_part(E0T, way, 1, 4, True), strip_part(E0T, way, 1, 4, False)))
    for way in diagonal:
        second.append(message(way, strip_part(E0T, way, 1, 3, True), strip_part(E0T, way, 1, 3, False)))
    for way in len_ways:
        second.append(message(way, nat_part(E0, way, 4, True), nat_part(E0, way, 4, False)))

    for side in range(2):
        for col in range(4, 6) if side == 0 else range(26, 28):
            for h in range(2):
                E0T[side, col - FIRST[side], h, own_t, :] = column(E0, h, NAT0, col)

    E = (E0, E1, E2, E3)
    ET = (E0T, E1T, E2T, E3T)

    def sweep_row(k, r):
        o = pl.multiple_of(32 * r, 32)
        src = E[k]
        x = [src[h, pl.ds(o, 32), :] for h in range(2)]
        xu, xd = k_up(x, False), k_down(x, False)
        for h in range(2):
            def t(q):
                return TN[q, h, pl.ds(o, 32), :]
            total = ALPHAS[k] * x[h] + t(4) * xd[h] + t(5) * xu[h]
            total = total + t(0) * src[h, pl.ds(o - 32, 32), :] + t(1) * src[h, pl.ds(o + 32, 32), :]
            total = total + t(2) * src[h, pl.ds(o - 1, 32), :] + t(3) * src[h, pl.ds(o + 1, 32), :]
            if k > 0:
                total = total + BETAS[k] * E[k - 1][h, pl.ds(o, 32), :]
            E[k + 1][h, pl.ds(o, 32), :] = total

    def sweep(k, first, last):
        def step(r, carry):
            sweep_row(k, r)
            return carry
        lax.fori_loop(first + DEEP, last + 1 + DEEP, step, 0, unroll=4)

    def potential_row(i, guess):
        o = pl.multiple_of(NAT0 + 32 * i, 32)
        q = pl.multiple_of(PW * (i + DEEP) + 8, 8)
        for h in range(2):
            total = guess(h)
            for k in range(SWEEPS):
                total = total + GAINS[k] * E[k][h, pl.ds(o, 32), :]
            POT[h, pl.ds(q, 32), :] = total

    def own_potential(first, last):
        def step(i, carry):
            p = pl.multiple_of(PAD + 32 * i, 8)
            potential_row(i, lambda h: G[h, pl.ds(p, 32), :])
            return carry
        lax.fori_loop(first, last + 1, step, 0, unroll=2)

    sweep(0, 1, 30)
    sweep(1, 2, 29)
    sweep(2, 3, 28)
    own_potential(3, 28)

    def force(i, carry):
        n = pl.multiple_of(32 * i, 32)
        o, p = pl.multiple_of(NAT0 + n, 32), pl.multiple_of(PAD + n, 8)
        for h in range(2):
            at = (h, pl.ds(n, 32), slice(None))
            cb = C[h, pl.ds(o, 32), :] * B[at]
            U0[at] = U0[at] + cb * HW[h, pl.ds(p, 32), :]
            U1[at] = U1[at] - cb * HL[at]
            B[at] = 0.25 * cb
        return carry

    lax.fori_loop(0, 32, force, 0)

    received(later_len)
    received(later_wid)
    received(later_diag)
    for i in (-3, -2, -1):
        row(i, has[-1, 0])
        row(31 - i, has[1, 0])
    for side in range(2):
        for col in range(0, 6) if side == 0 else range(26, 32):
            c = col - FIRST[side]
            for h in range(2):
                CT[side, c, h, pl.ds(12, 4), :] = column(C, h, 0, col, 4)
                CT[side, c, h, pl.ds(48, 4), :] = column(C, h, NAT0 + 1024, col, 4)
                KT[side, c, h, pl.ds(13, 3), :] = column(K, h, 32, col, 3)
                KT[side, c, h, pl.ds(48, 3), :] = column(K, h, NAT0 + 1024, col, 3)

    ii = lax.broadcasted_iota(jnp.int32, (40, 128), 0)
    rows_in = jnp.logical_and(
        jnp.logical_or(ii >= 4, has[-1, 0]), jnp.logical_or(ii < 36, has[1, 0])
    )

    for side in range(2):
        has_side = has[0, -1 if side == 0 else 1]

        def strip(c, carry):
            x = [CT[side, c, h, TAREA, :] for h in range(2)]
            cu, cd = k_up(x, True), k_down(x, True)
            in_own = c >= 4 if side == 0 else c < 6
            valid = jnp.logical_and(rows_in, jnp.logical_or(in_own, has_side))
            for h in range(2):
                slm = 0.5 * (x[h] + CT[side, c, h, pl.ds(11, 40), :])
                slp = 0.5 * (x[h] + CT[side, c, h, pl.ds(13, 40), :])
                swm = 0.5 * (x[h] + CT[side, c - 1, h, TAREA, :])
                swp = 0.5 * (x[h] + CT[side, c + 1, h, TAREA, :])
                skm, skp = 0.5 * (x[h] + cd[h]), 0.5 * (x[h] + cu[h])
                diag = 2.0 * KT[side, c, h, TAREA, :] + ((slm + slp) + (swm + swp)) + (skm + skp)
                iv = jnp.where(valid, 1.0 / diag, 0.0)

                def store(q, t):
                    TT[q, side, c, h, TAREA, :] = t

                put_coefficients(iv, h, (slm, slp, swm, swp, skm, skp), store)
            return carry

        for c in range(1, 9):
            strip(c, 0)

    received(second)

    for side in range(2):
        for col in range(0, 6) if side == 0 else range(26, 32):
            c = col - FIRST[side]
            for h in range(2):
                E0T[side, c, h, pl.ds(12, 4), :] = column(E0, h, 0, col, 4)
                E0T[side, c, h, pl.ds(48, 4), :] = column(E0, h, NAT0 + 1024, col, 4)

    for k in range(SWEEPS - 1):
        for side in range(2):
            def strip_sweep(c, carry):
                src = ET[k]
                x = [src[side, c, h, TAREA, :] for h in range(2)]
                xu, xd = k_up(x, False), k_down(x, False)
                for h in range(2):
                    def t(q):
                        return TT[q, side, c, h, TAREA, :]
                    total = ALPHAS[k] * x[h] + t(4) * xd[h] + t(5) * xu[h]
                    total = total + t(0) * src[side, c, h, pl.ds(11, 40), :] + t(1) * src[side, c, h, pl.ds(13, 40), :]
                    total = total + t(2) * src[side, c - 1, h, TAREA, :] + t(3) * src[side, c + 1, h, TAREA, :]
                    if k > 0:
                        total = total + BETAS[k] * ET[k - 1][side, c, h, TAREA, :]
                    ET[k + 1][side, c, h, TAREA, :] = total
                return carry

            for c in range(1 + k, 9 - k):
                strip_sweep(c, 0)
        sweep(k, k - 3, k)
        sweep(k, 31 - k, 34 - k)

    own_potential(0, 2)
    own_potential(29, 31)
    potential_row(-1, lambda h: GH[0, h])
    potential_row(32, lambda h: GH[1, h])
    for side in range(2):
        for c in range(3, 7):
            col = c + FIRST[side]
            for h in range(2):
                if 0 <= col < 32:
                    GT[side, c, h, pl.ds(15, 1), :] = GH[0, h, pl.ds(col, 1), :]
                    GT[side, c, h, pl.ds(48, 1), :] = GH[1, h, pl.ds(col, 1), :]
                total = GT[side, c, h, TAREA, :]
                for k in range(SWEEPS):
                    total = total + GAINS[k] * ET[k][side, c, h, TAREA, :]
                POT[h, pl.ds(8 + col, 40, stride=PW), :] = total

    def finish(i, carry):
        n = pl.multiple_of(32 * i, 32)
        q = pl.multiple_of(PW * (i + DEEP) + 8, 8)
        for h in range(2):
            at = (h, pl.ds(n, 32), slice(None))
            lanes = pl.ds(128 * h, 128)
            pot_out[pl.ds(n, 32), lanes] = POT[h, pl.ds(q, 32), :]
            vel_out[0, pl.ds(n, 32), lanes] = U0[at] - B[at] * (
                POT[h, pl.ds(q + 1, 32), :] - POT[h, pl.ds(q - 1, 32), :]
            )
            vel_out[1, pl.ds(n, 32), lanes] = U1[at] + B[at] * (
                POT[h, pl.ds(q + PW, 32), :] - POT[h, pl.ds(q - PW, 32), :]
            )
        return carry

    lax.fori_loop(0, 32, finish, 0, unroll=2)

    for way, copy in sent:
        @pl.when(has[way])
        def _():
            copy.wait_send()


N_MESSAGES = 34


def solution(mesh):
    n_len, n_wid = mesh.shape["len"], mesh.shape["wid"]

    def body(velocity, bfield, material, wall_mask, potential_guess):
        flat = lambda a: pltpu.with_memory_space_constraint(a.reshape(a.shape[:-3] + (1024, 256)), pltpu.HBM)
        own = pltpu.VMEM((2, 1024, 128), jnp.float32)
        padded = pltpu.VMEM((2, 1024 + 2 * PAD, 128), jnp.float32)
        nat = pltpu.VMEM((2, 1024 + 2 * NAT0, 128), jnp.float32)
        strip = pltpu.VMEM((2, 10, 2, TROWS, 128), jnp.float32)
        ints = pltpu.VMEM((2, 1024, 128), jnp.int32)
        rows = pltpu.VMEM((2, 2, 32, 128), jnp.float32)
        scratch = [
            own, own, own, ints, ints, padded, own, padded, nat, nat, nat, nat, own, own, nat, nat, nat, nat,
            pltpu.VMEM((6, 2, 1024 + 2 * NAT0, 128), jnp.float32), rows,
            strip, strip, strip, rows, rows, strip, strip, strip, strip,
            pltpu.VMEM((6, 2, 10, 2, TROWS, 128), jnp.float32),
            pltpu.VMEM((2, 40 * PW, 128), jnp.float32),
            pltpu.SemaphoreType.DMA((12,)),
            pltpu.SemaphoreType.DMA((N_MESSAGES,)),
            pltpu.SemaphoreType.DMA((N_MESSAGES,)),
        ]
        vel, pot = pl.pallas_call(
            functools.partial(kernel, n_len, n_wid),
            out_shape=(
                pltpu.VMEM((2, 1024, 256), jnp.float32),
                pltpu.VMEM((1024, 256), jnp.float32),
            ),
            in_specs=[pl.BlockSpec(memory_space=pltpu.HBM)] * 5,
            out_specs=(pl.BlockSpec(memory_space=pltpu.VMEM), pl.BlockSpec(memory_space=pltpu.VMEM)),
            scratch_shapes=scratch,
            compiler_params=pltpu.CompilerParams(
                collective_id=0, has_side_effects=True, vmem_limit_bytes=50 * 1024 * 1024
            ),
        )(flat(velocity), flat(bfield), flat(material), flat(wall_mask), flat(potential_guess))
        return vel.reshape(velocity.shape), pot.reshape(bfield.shape)

    whole, part = P(None, "len", "wid", None), P("len", "wid", None)
    return jax.shard_map(
        body,
        mesh=mesh,
        in_specs=(whole, part, part, part, part),
        out_specs=(whole, part),
        check_vma=False,
    )
```

```python
import functools

import jax
import jax.numpy as jnp
from jax import lax
from jax.experimental import pallas as pl
from jax.experimental.pallas import tpu as pltpu
from jax.sharding import PartitionSpec as P

MESH = pl.DeviceIdType.MESH
SWEEPS = 4
THETA = 0.5 * (2.0 + 0.1)
DELTA = 0.5 * (2.0 - 0.1)
S1 = THETA / DELTA

ROWS = 32
DEEP = 4
NAT0 = DEEP * 32
PAD = 8
TROWS = 64
TOWN = 16
TAREA = pl.ds(12, 40)
PW = 48
FIRST = (-4, 26)
OWN_COLS = (range(0, 4), range(28, 32))


def chebyshev():
    weight = 1.0 / S1
    gains, alphas, betas = [1.0 / THETA], [], []
    kf_old = nf_old = None
    for _ in range(SWEEPS - 1):
        weight_next = 1.0 / (2.0 * S1 - weight)
        kf, nf = weight_next * weight, 2.0 * weight_next / DELTA
        if nf_old is None:
            alphas.append(kf / nf + THETA - 1.0)
            betas.append(0.0)
        else:
            alphas.append(kf / nf + 1.0 / nf_old - 1.0)
            betas.append(-kf_old / (nf_old * nf_old))
        gains.append(nf * gains[-1])
        kf_old, nf_old, weight = kf, nf, weight_next
    return gains, alphas, betas


GAINS, ALPHAS, BETAS = chebyshev()


def lanes_of(shape):
    return lax.broadcasted_iota(jnp.int32, shape, 1)


def k_up(x, zero):
    r = [pltpu.roll(v, 127, 1) for v in x]
    last = lanes_of(x[0].shape) == 127
    return [jnp.where(last, r[1], r[0]), jnp.where(last, 0.0, r[1]) if zero else r[1]]


def k_down(x, zero):
    r = [pltpu.roll(v, 1, 1) for v in x]
    first = lanes_of(x[0].shape) == 0
    return [jnp.where(first, 0.0, r[0]) if zero else r[0], jnp.where(first, r[0], r[1])]


def kernel(n_len, n_wid, u_hbm, b_hbm, m_hbm, w_hbm, g_hbm, vel_out, pot_out,
           U0, U1, B, MAT, WALL, G, HL, HW, QP, QM, C, K, RP, DP, E0, E1, E2, TN, GH,
           CT, KT, GT, QS, QR, E0T, E1T, E2T, E3T, TT, POT, lsem, ssem, rsem):
    li, wi = lax.axis_index("len"), lax.axis_index("wid")
    has = {(-1, 0): li > 0, (1, 0): li < n_len - 1, (0, -1): wi > 0, (0, 1): wi < n_wid - 1}
    for dl in (-1, 1):
        for dw in (-1, 1):
            has[dl, dw] = jnp.logical_and(has[dl, 0], has[0, dw])
    straight = ((0, -1), (0, 1), (-1, 0), (1, 0))
    diagonal = ((-1, -1), (-1, 1), (1, -1), (1, 1))

    barrier = pltpu.get_barrier_semaphore()
    for way in straight:
        @pl.when(has[way])
        def _():
            pl.semaphore_signal(barrier, inc=1, device_id=(li + way[0], wi + way[1]), device_id_type=MESH)

    own = pl.ds(PAD, 1024)
    loads = []
    for src, dst in (
        (m_hbm, lambda h: MAT.at[h]), (u_hbm.at[0], lambda h: U0.at[h]), (b_hbm, lambda h: B.at[h]),
        (g_hbm, lambda h: G.at[h, own]), (u_hbm.at[1], lambda h: U1.at[h]), (w_hbm, lambda h: WALL.at[h]),
    ):
        for h in range(2):
            copy = pltpu.make_async_copy(src.at[:, pl.ds(128 * h, 128)], dst(h), lsem.at[len(loads)])
            copy.start()
            loads.append(copy)

    for dl in (-1, 1):
        rows = pl.ds(0, 128) if dl < 0 else pl.ds(NAT0 + 1024, 128)
        @pl.when(jnp.logical_not(has[dl, 0]))
        def _():
            for ref in (C, K, E0, QP, QM):
                for h in range(2):
                    ref[h, rows, :] = jnp.zeros((128, 128), jnp.float32)
            for h in range(2):
                GH[(dl + 1) // 2, h] = jnp.zeros((32, 128), jnp.float32)
    for dw in (-1, 1):
        side = (dw + 1) // 2
        c0 = 0 if dw < 0 else 6
        @pl.when(jnp.logical_not(has[0, dw]))
        def _():
            for h in range(2):
                QR[side, h] = jnp.zeros((32, 128), jnp.float32)
                for c in range(c0, c0 + 4):
                    for ref in (CT, KT, GT, E0T):
                        ref[side, c, h, pl.ds(TOWN, 32), :] = jnp.zeros((32, 128), jnp.float32)
    for dl, dw in diagonal:
        side = (dw + 1) // 2
        c0 = 0 if dw < 0 else 6
        @pl.when(jnp.logical_not(has[dl, dw]))
        def _():
            for h in range(2):
                for c in range(c0, c0 + 4):
                    for ref in (CT, KT, E0T):
                        ref[side, c, h, pl.ds(8 if dl < 0 else 48, 8), :] = jnp.zeros((8, 128), jnp.float32)

    def column(ref, h, first, col, rows=32):
        return ref[h, pl.ds(first + col, rows, stride=32), :]

    def conduct(m):
        return jnp.where(m == 0, 1.0, jnp.where(m == 1, 0.5, 6.0))

    own_t = pl.ds(TOWN, 32)
    edges = ((0, 0, 4, -1.0), (1, 31, 5, 1.0))
    for copy in loads[:8]:
        copy.wait()
    for side, col, c, sign in edges:
        for h in range(2):
            g = column(G, h, PAD, col)
            CT[side, c, h, own_t, :] = conduct(column(MAT, h, 0, col))
            GT[side, c, h, own_t, :] = g
            QS[side, h] = g - sign * (0.5 * (column(U0, h, 0, col) * column(B, h, 0, col)))
    for copy in loads[8:]:
        copy.wait()

    def prepare(i, carry):
        n = pl.multiple_of(32 * i, 32)
        o, p = pl.multiple_of(NAT0 + n, 32), pl.multiple_of(PAD + n, 8)
        for h in range(2):
            m = MAT[h, pl.ds(n, 32), :]
            b, g = B[h, pl.ds(n, 32), :], G[h, pl.ds(p, 32), :]
            hl = 0.5 * (U1[h, pl.ds(n, 32), :] * b)
            C[h, pl.ds(o, 32), :] = conduct(m)
            K[h, pl.ds(o, 32), :] = WALL[h, pl.ds(n, 32), :].astype(jnp.float32)
            HL[h, pl.ds(n, 32), :] = hl
            HW[h, pl.ds(p, 32), :] = -0.5 * (U0[h, pl.ds(n, 32), :] * b)
            QP[h, pl.ds(o, 32), :] = g + hl
            QM[h, pl.ds(o, 32), :] = g - hl
        return carry

    lax.fori_loop(0, 32, prepare, 0, unroll=4)

    sent = []

    def message(way, src, dst):
        k = len(sent)
        copy = pltpu.make_async_remote_copy(
            src, dst, ssem.at[k], rsem.at[k], device_id=(li + way[0], wi + way[1]), device_id_type=MESH
        )
        sent.append((way, copy))
        @pl.when(has[way])
        def _():
            copy.start()
        return way, copy

    def received(messages):
        for way, copy in messages:
            @pl.when(has[-way[0], -way[1]])
            def _():
                copy.wait_recv()

    def nat_part(ref, way, depth, here):
        if way[0] < 0:
            first = NAT0 if here else NAT0 + 1024
        else:
            first = NAT0 + 1024 - 32 * depth if here else NAT0 - 32 * depth
        return ref.at[:, pl.ds(first, 32 * depth), :]

    def strip_part(ref, way, near, far, here):
        count = far - near + 1
        if way[1] < 0:
            side, first = (0, 3 + near) if here else (1, 5 + near)
        else:
            side, first = (1, 6 - far) if here else (0, 4 - far)
        if way[0] == 0:
            rows = own_t
        elif way[0] < 0:
            rows = pl.ds(16 if here else 48, 4)
        else:
            rows = pl.ds(44 if here else 12, 4)
        return ref.at[side, pl.ds(first, count), :, rows, :]

    pl.semaphore_wait(barrier, sum(has[way].astype(jnp.int32) for way in straight))

    wid_ways, len_ways = straight[:2], straight[2:]
    first_wid, first_len, later_len, later_wid = [], [], [], []
    for way in wid_ways:
        out, into = (0, 1) if way[1] < 0 else (1, 0)
        first_wid.append(message(way, QS.at[out], QR.at[into]))
        first_wid.append(message(way, strip_part(CT, way, 1, 1, True), strip_part(CT, way, 1, 1, False)))
    for way in len_ways:
        Q = QM if way[0] < 0 else QP
        first_len.append(message(way, nat_part(Q, way, 1, True), nat_part(Q, way, 1, False)))
        first_len.append(message(way, nat_part(C, way, 4, True), nat_part(C, way, 4, False)))
    for side in range(2):
        for col in OWN_COLS[side]:
            c = col - FIRST[side]
            for h in range(2):
                if col not in (0, 31):
                    CT[side, c, h, own_t, :] = column(C, h, NAT0, col)
                    if 3 <= c <= 6:
                        GT[side, c, h, own_t, :] = column(G, h, PAD, col)
                KT[side, c, h, own_t, :] = column(K, h, NAT0, col)
    for way in wid_ways:
        later_wid.append(message(way, strip_part(CT, way, 2, 4, True), strip_part(CT, way, 2, 4, False)))
        later_wid.append(message(way, strip_part(KT, way, 1, 3, True), strip_part(KT, way, 1, 3, False)))
        later_wid.append(message(way, strip_part(GT, way, 1, 1, True), strip_part(GT, way, 1, 1, False)))
    for way in len_ways:
        into = 1 if way[0] < 0 else 0
        first = PAD if way[0] < 0 else PAD + 31 * 32
        later_len.append(message(way, nat_part(K, way, 3, True), nat_part(K, way, 3, False)))
        later_len.append(message(way, G.at[:, pl.ds(first, 32), :], GH.at[into]))

    shape = (32, 128)
    jj = lax.broadcasted_iota(jnp.int32, shape, 0)
    lane = lanes_of(shape)

    def put_coefficients(iv, h, s, store):
        for q in range(6):
            t = s[q] * iv
            if q == 4 and h == 0:
                t = jnp.where(lanes_of(t.shape) == 0, 0.0, t)
            if q == 5 and h == 1:
                t = jnp.where(lanes_of(t.shape) == 127, 0.0, t)
            store(q, t)

    def row(i, valid=None):
        n = pl.multiple_of(32 * i, 32)
        o = pl.multiple_of(NAT0 + n, 32)
        p = pl.multiple_of(PAD + n, 8)
        c = [C[h, pl.ds(o, 32), :] for h in range(2)]
        cu, cd = k_up(c, True), k_down(c, True)
        if valid is None:
            g = [G[h, pl.ds(p, 32), :] for h in range(2)]
            gu, gd = k_up(g, True), k_down(g, True)
        for h in range(2):
            slm = 0.5 * (c[h] + C[h, pl.ds(o - 32, 32), :])
            slp = 0.5 * (c[h] + C[h, pl.ds(o + 32, 32), :])
            swm = jnp.where(jj == 0, 0.0, 0.5 * (c[h] + C[h, pl.ds(o - 1, 32), :]))
            swp = jnp.where(jj == 31, 0.0, 0.5 * (c[h] + C[h, pl.ds(o + 1, 32), :]))
            skm, skp = 0.5 * (c[h] + cd[h]), 0.5 * (c[h] + cu[h])
            k2 = 2.0 * K[h, pl.ds(o, 32), :]
            diag = k2 + ((slm + slp) + (swm + swp)) + (skm + skp)
            iv = 1.0 / diag
            if valid is None:
                hl, hw = HL[h, pl.ds(n, 32), :], HW[h, pl.ds(p, 32), :]
                gwm = jnp.where(jj == 0, 0.0, G[h, pl.ds(p - 1, 32), :] + HW[h, pl.ds(p - 1, 32), :] + hw)
                gwp = jnp.where(jj == 31, 0.0, G[h, pl.ds(p + 1, 32), :] - HW[h, pl.ds(p + 1, 32), :] - hw)
                res = slm * (QP[h, pl.ds(o - 32, 32), :] + hl) + slp * (QM[h, pl.ds(o + 32, 32), :] - hl)
                res = res + (swm * gwm + swp * gwp) + (skm * gd[h] + skp * gu[h]) - diag * g[h]
                at = (h, pl.ds(n, 32), slice(None))
                cb = c[h] * B[at]
                U0[at] = U0[at] + cb * hw
                U1[at] = U1[at] - cb * hl
                B[at] = 0.25 * cb
                RP[h, pl.ds(n, 32), :] = res
                DP[h, pl.ds(n, 32), :] = diag
                E0[h, pl.ds(o, 32), :] = res * iv
            else:
                iv = jnp.where(valid, iv, 0.0)

            def store(q, t):
                TN[q, h, pl.ds(o, 32), :] = t

            put_coefficients(iv, h, (slm, slp, swm, swp, skm, skp), store)

    def row_step(i, carry):
        row(i)
        return carry

    lax.fori_loop(1, 31, row_step, 0, unroll=5)

    received(first_len)
    row(0)
    row(31)
    later_diag = []
    for way in diagonal:
        later_diag.append(message(way, strip_part(CT, way, 1, 3, True), strip_part(CT, way, 1, 3, False)))
        later_diag.append(message(way, strip_part(KT, way, 1, 2, True), strip_part(KT, way, 1, 2, False)))

    for side in range(2):
        for col in OWN_COLS[side]:
            if col not in (0, 31):
                for h in range(2):
                    E0T[side, col - FIRST[side], h, own_t, :] = column(E0, h, NAT0, col)
    second, second_len = [], []
    for way in wid_ways:
        second.append(message(way, strip_part(E0T, way, 2, 4, True), strip_part(E0T, way, 2, 4, False)))

    received(first_wid)
    for side, col, c, sign in edges:
        halo = c - 1 if side == 0 else c + 1
        for h in range(2):
            s = 0.5 * (CT[side, c, h, own_t, :] + CT[side, halo, h, own_t, :])
            res = column(RP, h, 0, col) + s * (
                QR[side, h] - sign * column(HW, h, PAD, col) - GT[side, c, h, own_t, :]
            )
            e = res / (column(DP, h, 0, col) + s)
            E0T[side, c, h, own_t, :] = e
            E0[h, pl.ds(NAT0 + col, 32, stride=32), :] = e
    for way in wid_ways:
        second.append(message(way, strip_part(E0T, way, 1, 1, True), strip_part(E0T, way, 1, 1, False)))
    for way in diagonal:
        second.append(message(way, strip_part(E0T, way, 1, 3, True), strip_part(E0T, way, 1, 3, False)))
    for way in len_ways:
        second_len.append(message(way, nat_part(E0, way, 4, True), nat_part(E0, way, 4, False)))

    E = (E0, E1, E2)
    ET = (E0T, E1T, E2T, E3T)

    def sweep_row(k, r, guess=None):
        o = pl.multiple_of(32 * r, 32)
        src = E[k]
        x = [src[h, pl.ds(o, 32), :] for h in range(2)]
        xu, xd = k_up(x, False), k_down(x, False)
        for h in range(2):
            def t(q):
                return TN[q, h, pl.ds(o, 32), :]
            total = ALPHAS[k] * x[h] + t(4) * xd[h] + t(5) * xu[h]
            total = total + t(0) * src[h, pl.ds(o - 32, 32), :] + t(1) * src[h, pl.ds(o + 32, 32), :]
            total = total + t(2) * src[h, pl.ds(o - 1, 32), :] + t(3) * src[h, pl.ds(o + 1, 32), :]
            if k > 0:
                old = E[k - 1][h, pl.ds(o, 32), :]
                total = total + BETAS[k] * old
            if k < SWEEPS - 2:
                E[k + 1][h, pl.ds(o, 32), :] = total
            else:
                g = guess(h) if guess else G[h, pl.ds(pl.multiple_of(o - (NAT0 - PAD), 8), 32), :]
                pot = (g + GAINS[0] * E0[h, pl.ds(o, 32), :]) + GAINS[1] * old
                pot = (pot + GAINS[2] * x[h]) + GAINS[3] * total
                POT[h, pl.ds(pl.multiple_of(PW * r + 8, 8), 32), :] = pot

    def sweep(k, first, last, unroll):
        def step(r, carry):
            sweep_row(k, r)
            return carry
        lax.fori_loop(first + DEEP, last + 1 + DEEP, step, 0, unroll=unroll)

    sweep(0, 1, 30, 10)
    sweep(1, 2, 29, 14)
    sweep(2, 3, 28, 13)

    received(later_len)
    received(later_wid)
    for i in (-3, -2, -1):
        row(i, has[-1, 0])
        row(31 - i, has[1, 0])
    for side in range(2):
        for col in OWN_COLS[side]:
            c = col - FIRST[side]
            for h in range(2):
                CT[side, c, h, pl.ds(12, 4), :] = column(C, h, 0, col, 4)
                CT[side, c, h, pl.ds(48, 4), :] = column(C, h, NAT0 + 1024, col, 4)
                if 3 <= c <= 6:
                    KT[side, c, h, pl.ds(13, 3), :] = column(K, h, 32, col, 3)
                    KT[side, c, h, pl.ds(48, 3), :] = column(K, h, NAT0 + 1024, col, 3)
                    GT[side, c, h, pl.ds(15, 1), :] = GH[0, h, pl.ds(col, 1), :]
                    GT[side, c, h, pl.ds(48, 1), :] = GH[1, h, pl.ds(col, 1), :]

    received(second_len)
    for k in range(SWEEPS - 1):
        for i in (*range(k - 3, k + 1), *range(31 - k, 35 - k)):
            guess = None
            if i == -1:
                guess = lambda h: GH[0, h]
            if i == 32:
                guess = lambda h: GH[1, h]
            sweep_row(k, i + DEEP, guess)
    for side in range(2):
        for col in OWN_COLS[side]:
            c = col - FIRST[side]
            for h in range(2):
                E0T[side, c, h, pl.ds(12, 4), :] = column(E0, h, 0, col, 4)
                E0T[side, c, h, pl.ds(48, 4), :] = column(E0, h, NAT0 + 1024, col, 4)
                if col in (1, 2, 29, 30):
                    E1T[side, c, h, TAREA, :] = column(E1, h, 0, col, 40)
                if col in (2, 3, 28, 29):
                    E2T[side, c, h, TAREA, :] = column(E2, h, 0, col, 40)

    def finish(first, count, unroll):
        def step(i, carry):
            n = pl.multiple_of(32 * i + first, 8)
            q = pl.multiple_of(PW * (i + DEEP) + 8 + first, 8)
            for h in range(2):
                at = (h, pl.ds(n, count), slice(None))
                lanes = pl.ds(128 * h, 128)
                pot_out[pl.ds(n, count), lanes] = POT[h, pl.ds(q, count), :]
                vel_out[0, pl.ds(n, count), lanes] = U0[at] - B[at] * (
                    POT[h, pl.ds(q + 1, count), :] - POT[h, pl.ds(q - 1, count), :]
                )
                vel_out[1, pl.ds(n, count), lanes] = U1[at] + B[at] * (
                    POT[h, pl.ds(q + PW, count), :] - POT[h, pl.ds(q - PW, count), :]
                )
            return carry

        lax.fori_loop(0, 32, step, 0, unroll=unroll)

    finish(8, 16, 4)
    received(later_diag)

    ii = lax.broadcasted_iota(jnp.int32, (40, 128), 0)
    rows_in = jnp.logical_and(
        jnp.logical_or(ii >= 4, has[-1, 0]), jnp.logical_or(ii < 36, has[1, 0])
    )

    for side in range(2):
        has_side = has[0, -1 if side == 0 else 1]

        def strip(c, carry):
            x = [CT[side, c, h, TAREA, :] for h in range(2)]
            cu, cd = k_up(x, True), k_down(x, True)
            in_own = c >= 4 if side == 0 else c < 6
            valid = jnp.logical_and(rows_in, jnp.logical_or(in_own, has_side))
            for h in range(2):
                slm = 0.5 * (x[h] + CT[side, c, h, pl.ds(11, 40), :])
                slp = 0.5 * (x[h] + CT[side, c, h, pl.ds(13, 40), :])
                swm = 0.5 * (x[h] + CT[side, c - 1, h, TAREA, :])
                swp = 0.5 * (x[h] + CT[side, c + 1, h, TAREA, :])
                skm, skp = 0.5 * (x[h] + cd[h]), 0.5 * (x[h] + cu[h])
                diag = 2.0 * KT[side, c, h, TAREA, :] + ((slm + slp) + (swm + swp)) + (skm + skp)
                iv = jnp.where(valid, 1.0 / diag, 0.0)

                def store(q, t):
                    TT[q, side, c, h, TAREA, :] = t

                put_coefficients(iv, h, (slm, slp, swm, swp, skm, skp), store)
            return carry

        for c in range(1, 7) if side == 0 else range(3, 9):
            strip(c, 0)

    received(second)

    for k in range(SWEEPS - 1):
        for side in range(2):
            def strip_sweep(c, carry):
                src = ET[k]
                x = [src[side, c, h, TAREA, :] for h in range(2)]
                xu, xd = k_up(x, False), k_down(x, False)
                for h in range(2):
                    def t(q):
                        return TT[q, side, c, h, TAREA, :]
                    total = ALPHAS[k] * x[h] + t(4) * xd[h] + t(5) * xu[h]
                    total = total + t(0) * src[side, c, h, pl.ds(11, 40), :] + t(1) * src[side, c, h, pl.ds(13, 40), :]
                    total = total + t(2) * src[side, c - 1, h, TAREA, :] + t(3) * src[side, c + 1, h, TAREA, :]
                    if k > 0:
                        total = total + BETAS[k] * ET[k - 1][side, c, h, TAREA, :]
                    ET[k + 1][side, c, h, TAREA, :] = total
                return carry

            for c in range(1 + k, 5 + k) if side == 0 else range(5 - k, 9 - k):
                strip_sweep(c, 0)

    for side in range(2):
        for c in range(3, 7):
            for h in range(2):
                total = GT[side, c, h, TAREA, :]
                for k in range(SWEEPS):
                    total = total + GAINS[k] * ET[k][side, c, h, TAREA, :]
                POT[h, pl.ds(8 + c + FIRST[side], 40, stride=PW), :] = total
    finish(0, 8, 4)
    finish(24, 8, 4)

    for way, copy in sent:
        @pl.when(has[way])
        def _():
            copy.wait_send()


N_MESSAGES = 36


def solution(mesh):
    n_len, n_wid = mesh.shape["len"], mesh.shape["wid"]

    def body(velocity, bfield, material, wall_mask, potential_guess):
        flat = lambda a: pltpu.with_memory_space_constraint(a.reshape(a.shape[:-3] + (1024, 256)), pltpu.HBM)
        own = pltpu.VMEM((2, 1024, 128), jnp.float32)
        padded = pltpu.VMEM((2, 1024 + 2 * PAD, 128), jnp.float32)
        nat = pltpu.VMEM((2, 1024 + 2 * NAT0, 128), jnp.float32)
        strip = pltpu.VMEM((2, 10, 2, TROWS, 128), jnp.float32)
        ints = pltpu.VMEM((2, 1024, 128), jnp.int32)
        rows = pltpu.VMEM((2, 2, 32, 128), jnp.float32)
        scratch = [
            own, own, own, ints, ints, padded, own, padded, nat, nat, nat, nat, own, own, nat, nat, nat,
            pltpu.VMEM((6, 2, 1024 + 2 * NAT0, 128), jnp.float32), rows,
            strip, strip, strip, rows, rows, strip, strip, strip, strip,
            pltpu.VMEM((6, 2, 10, 2, TROWS, 128), jnp.float32),
            pltpu.VMEM((2, 40 * PW, 128), jnp.float32),
            pltpu.SemaphoreType.DMA((12,)),
            pltpu.SemaphoreType.DMA((N_MESSAGES,)),
            pltpu.SemaphoreType.DMA((N_MESSAGES,)),
        ]
        vel, pot = pl.pallas_call(
            functools.partial(kernel, n_len, n_wid),
            out_shape=(
                pltpu.VMEM((2, 1024, 256), jnp.float32),
                pltpu.VMEM((1024, 256), jnp.float32),
            ),
            in_specs=[pl.BlockSpec(memory_space=pltpu.HBM)] * 5,
            out_specs=(pl.BlockSpec(memory_space=pltpu.VMEM), pl.BlockSpec(memory_space=pltpu.VMEM)),
            scratch_shapes=scratch,
            compiler_params=pltpu.CompilerParams(
                collective_id=0, has_side_effects=True, vmem_limit_bytes=50 * 1024 * 1024
            ),
        )(flat(velocity), flat(bfield), flat(material), flat(wall_mask), flat(potential_guess))
        return vel.reshape(velocity.shape), pot.reshape(bfield.shape)

    whole, part = P(None, "len", "wid", None), P("len", "wid", None)
    return jax.shard_map(
        body,
        mesh=mesh,
        in_specs=(whole, part, part, part, part),
        out_specs=(whole, part),
        check_vma=False,
    )
```

```python
import functools

import jax
import jax.numpy as jnp
from jax import lax
from jax.experimental import pallas as pl
from jax.experimental.pallas import tpu as pltpu
from jax.sharding import PartitionSpec as P

MESH = pl.DeviceIdType.MESH
SWEEPS = 4
THETA = 0.5 * (2.0 + 0.1)
DELTA = 0.5 * (2.0 - 0.1)
S1 = THETA / DELTA

ROWS = 32
DEEP = 4
NAT0 = DEEP * 32
PAD = 8
TROWS = 64
TOWN = 16
TAREA = pl.ds(12, 40)
PW = 48
FIRST = (-4, 26)
OWN_COLS = (range(0, 4), range(28, 32))


def chebyshev():
    weight = 1.0 / S1
    gains, alphas, betas = [1.0 / THETA], [], []
    kf_old = nf_old = None
    for _ in range(SWEEPS - 1):
        weight_next = 1.0 / (2.0 * S1 - weight)
        kf, nf = weight_next * weight, 2.0 * weight_next / DELTA
        if nf_old is None:
            alphas.append(kf / nf + THETA - 1.0)
            betas.append(0.0)
        else:
            alphas.append(kf / nf + 1.0 / nf_old - 1.0)
            betas.append(-kf_old / (nf_old * nf_old))
        gains.append(nf * gains[-1])
        kf_old, nf_old, weight = kf, nf, weight_next
    return gains, alphas, betas


GAINS, ALPHAS, BETAS = chebyshev()


def lanes_of(shape):
    return lax.broadcasted_iota(jnp.int32, shape, 1)


def k_up(x, zero):
    r = [pltpu.roll(v, 127, 1) for v in x]
    last = lanes_of(x[0].shape) == 127
    return [jnp.where(last, r[1], r[0]), jnp.where(last, 0.0, r[1]) if zero else r[1]]


def k_down(x, zero):
    r = [pltpu.roll(v, 1, 1) for v in x]
    first = lanes_of(x[0].shape) == 0
    return [jnp.where(first, 0.0, r[0]) if zero else r[0], jnp.where(first, r[0], r[1])]


def kernel(n_len, n_wid, u_hbm, b_hbm, m_hbm, w_hbm, g_hbm, vel_out, pot_out,
           U0, U1, B, MAT, WALL, G, HL, HW, QP, QM, C, K, RP, DP, E0, E1, E2, TN, GH,
           CT, KT, GT, QS, QR, E0T, E1T, E2T, E3T, TT, POT, lsem, ssem, rsem):
    li, wi = lax.axis_index("len"), lax.axis_index("wid")
    has = {(-1, 0): li > 0, (1, 0): li < n_len - 1, (0, -1): wi > 0, (0, 1): wi < n_wid - 1}
    for dl in (-1, 1):
        for dw in (-1, 1):
            has[dl, dw] = jnp.logical_and(has[dl, 0], has[0, dw])
    straight = ((0, -1), (0, 1), (-1, 0), (1, 0))
    diagonal = ((-1, -1), (-1, 1), (1, -1), (1, 1))

    barrier = pltpu.get_barrier_semaphore()
    for way in straight:
        @pl.when(has[way])
        def _():
            pl.semaphore_signal(barrier, inc=1, device_id=(li + way[0], wi + way[1]), device_id_type=MESH)

    own = pl.ds(PAD, 1024)
    loads = []
    for src, dst in (
        (m_hbm, lambda h: MAT.at[h]), (u_hbm.at[0], lambda h: U0.at[h]), (b_hbm, lambda h: B.at[h]),
        (g_hbm, lambda h: G.at[h, own]), (u_hbm.at[1], lambda h: U1.at[h]), (w_hbm, lambda h: WALL.at[h]),
    ):
        for h in range(2):
            copy = pltpu.make_async_copy(src.at[:, pl.ds(128 * h, 128)], dst(h), lsem.at[len(loads)])
            copy.start()
            loads.append(copy)

    for dl in (-1, 1):
        rows = pl.ds(0, 128) if dl < 0 else pl.ds(NAT0 + 1024, 128)
        @pl.when(jnp.logical_not(has[dl, 0]))
        def _():
            for ref in (C, K, E0, QP, QM):
                for h in range(2):
                    ref[h, rows, :] = jnp.zeros((128, 128), jnp.float32)
            for h in range(2):
                GH[(dl + 1) // 2, h] = jnp.zeros((32, 128), jnp.float32)
    for dw in (-1, 1):
        side = (dw + 1) // 2
        c0 = 0 if dw < 0 else 6
        @pl.when(jnp.logical_not(has[0, dw]))
        def _():
            for h in range(2):
                for kind in range(2):
                    QR[side, kind, h] = jnp.zeros((32, 128), jnp.float32)
                for c in range(c0, c0 + 4):
                    for ref in (CT, KT, GT, E0T):
                        ref[side, c, h, pl.ds(TOWN, 32), :] = jnp.zeros((32, 128), jnp.float32)
    for dl, dw in diagonal:
        side = (dw + 1) // 2
        c0 = 0 if dw < 0 else 6
        @pl.when(jnp.logical_not(has[dl, dw]))
        def _():
            for h in range(2):
                for c in range(c0, c0 + 4):
                    for ref in (CT, KT, E0T):
                        ref[side, c, h, pl.ds(8 if dl < 0 else 48, 8), :] = jnp.zeros((8, 128), jnp.float32)

    def column(ref, h, first, col, rows=32):
        return ref[h, pl.ds(first + col, rows, stride=32), :]

    def conduct(m):
        return jnp.where(m == 0, 1.0, jnp.where(m == 1, 0.5, 6.0))

    own_t = pl.ds(TOWN, 32)
    edges = ((0, 0, 4, -1.0), (1, 31, 5, 1.0))
    for copy in loads[:8]:
        copy.wait()
    for side, col, c, sign in edges:
        for h in range(2):
            g = column(G, h, PAD, col)
            cond = conduct(column(MAT, h, 0, col))
            CT[side, c, h, own_t, :] = cond
            GT[side, c, h, own_t, :] = g
            QS[side, 1, h] = cond
            QS[side, 0, h] = g - sign * (0.5 * (column(U0, h, 0, col) * column(B, h, 0, col)))
    for copy in loads[8:]:
        copy.wait()

    def prepare(i, carry):
        n = pl.multiple_of(32 * i, 32)
        o, p = pl.multiple_of(NAT0 + n, 32), pl.multiple_of(PAD + n, 8)
        for h in range(2):
            m = MAT[h, pl.ds(n, 32), :]
            b, g = B[h, pl.ds(n, 32), :], G[h, pl.ds(p, 32), :]
            hl = 0.5 * (U1[h, pl.ds(n, 32), :] * b)
            C[h, pl.ds(o, 32), :] = conduct(m)
            K[h, pl.ds(o, 32), :] = WALL[h, pl.ds(n, 32), :].astype(jnp.float32)
            HL[h, pl.ds(n, 32), :] = hl
            HW[h, pl.ds(p, 32), :] = -0.5 * (U0[h, pl.ds(n, 32), :] * b)
            QP[h, pl.ds(o, 32), :] = g + hl
            QM[h, pl.ds(o, 32), :] = g - hl
        return carry

    lax.fori_loop(0, 32, prepare, 0, unroll=4)

    sent = []

    def message(way, src, dst):
        k = len(sent)
        copy = pltpu.make_async_remote_copy(
            src, dst, ssem.at[k], rsem.at[k], device_id=(li + way[0], wi + way[1]), device_id_type=MESH
        )
        sent.append((way, copy))
        @pl.when(has[way])
        def _():
            copy.start()
        return way, copy

    def received(messages):
        for way, copy in messages:
            @pl.when(has[-way[0], -way[1]])
            def _():
                copy.wait_recv()

    def nat_part(ref, way, depth, here, skip=0):
        if way[0] < 0:
            first = (NAT0 if here else NAT0 + 1024) + 32 * skip
        else:
            first = NAT0 + 1024 - 32 * depth if here else NAT0 - 32 * depth
        return ref.at[:, pl.ds(first, 32 * (depth - skip)), :]

    def strip_part(ref, way, near, far, here):
        count = far - near + 1
        if way[1] < 0:
            side, first = (0, 3 + near) if here else (1, 5 + near)
        else:
            side, first = (1, 6 - far) if here else (0, 4 - far)
        if way[0] == 0:
            rows = own_t
        elif way[0] < 0:
            rows = pl.ds(16 if here else 48, far)
        else:
            rows = pl.ds((48 if here else 16) - far, far)
        return ref.at[side, pl.ds(first, count), :, rows, :]

    pl.semaphore_wait(barrier, sum(has[way].astype(jnp.int32) for way in straight))

    wid_ways, len_ways = straight[:2], straight[2:]
    first_wid, first_len, later_len, later_wid, last = [], [], [], [], []
    for way in wid_ways:
        out, into = (0, 1) if way[1] < 0 else (1, 0)
        first_wid.append(message(way, QS.at[out], QR.at[into]))
    for way in len_ways:
        Q = QM if way[0] < 0 else QP
        first_len.append(message(way, nat_part(Q, way, 1, True), nat_part(Q, way, 1, False)))
        first_len.append(message(way, nat_part(C, way, 1, True), nat_part(C, way, 1, False)))
    for side in range(2):
        for col in OWN_COLS[side]:
            c = col - FIRST[side]
            for h in range(2):
                if col not in (0, 31):
                    CT[side, c, h, own_t, :] = column(C, h, NAT0, col)
                    if 3 <= c <= 6:
                        GT[side, c, h, own_t, :] = column(G, h, PAD, col)
                KT[side, c, h, own_t, :] = column(K, h, NAT0, col)

    shape = (32, 128)
    jj = lax.broadcasted_iota(jnp.int32, shape, 0)
    lane = lanes_of(shape)

    def put_coefficients(iv, h, s, store):
        for q in range(6):
            t = s[q] * iv
            if q == 4 and h == 0:
                t = jnp.where(lanes_of(t.shape) == 0, 0.0, t)
            if q == 5 and h == 1:
                t = jnp.where(lanes_of(t.shape) == 127, 0.0, t)
            store(q, t)

    def row(i, valid=None):
        n = pl.multiple_of(32 * i, 32)
        o = pl.multiple_of(NAT0 + n, 32)
        p = pl.multiple_of(PAD + n, 8)
        c = [C[h, pl.ds(o, 32), :] for h in range(2)]
        cu, cd = k_up(c, True), k_down(c, True)
        if valid is None:
            g = [G[h, pl.ds(p, 32), :] for h in range(2)]
            gu, gd = k_up(g, True), k_down(g, True)
        for h in range(2):
            slm = 0.5 * (c[h] + C[h, pl.ds(o - 32, 32), :])
            slp = 0.5 * (c[h] + C[h, pl.ds(o + 32, 32), :])
            swm = jnp.where(jj == 0, 0.0, 0.5 * (c[h] + C[h, pl.ds(o - 1, 32), :]))
            swp = jnp.where(jj == 31, 0.0, 0.5 * (c[h] + C[h, pl.ds(o + 1, 32), :]))
            skm, skp = 0.5 * (c[h] + cd[h]), 0.5 * (c[h] + cu[h])
            k2 = 2.0 * K[h, pl.ds(o, 32), :]
            diag = k2 + ((slm + slp) + (swm + swp)) + (skm + skp)
            iv = 1.0 / diag
            if valid is None:
                hl, hw = HL[h, pl.ds(n, 32), :], HW[h, pl.ds(p, 32), :]
                gwm = jnp.where(jj == 0, 0.0, G[h, pl.ds(p - 1, 32), :] + HW[h, pl.ds(p - 1, 32), :] + hw)
                gwp = jnp.where(jj == 31, 0.0, G[h, pl.ds(p + 1, 32), :] - HW[h, pl.ds(p + 1, 32), :] - hw)
                res = slm * (QP[h, pl.ds(o - 32, 32), :] + hl) + slp * (QM[h, pl.ds(o + 32, 32), :] - hl)
                res = res + (swm * gwm + swp * gwp) + (skm * gd[h] + skp * gu[h]) - diag * g[h]
                at = (h, pl.ds(n, 32), slice(None))
                cb = c[h] * B[at]
                U0[at] = U0[at] + cb * hw
                U1[at] = U1[at] - cb * hl
                B[at] = 0.25 * cb
                RP[h, pl.ds(n, 32), :] = res
                DP[h, pl.ds(n, 32), :] = diag
                E0[h, pl.ds(o, 32), :] = res * iv
            else:
                iv = jnp.where(valid, iv, 0.0)

            def store(q, t):
                TN[q, h, pl.ds(o, 32), :] = t

            put_coefficients(iv, h, (slm, slp, swm, swp, skm, skp), store)

    def row_step(i, carry):
        row(i)
        return carry

    for way in wid_ways:
        later_wid.append(message(way, strip_part(CT, way, 2, 4, True), strip_part(CT, way, 2, 4, False)))
        later_wid.append(message(way, strip_part(KT, way, 1, 3, True), strip_part(KT, way, 1, 3, False)))
    for way in len_ways:
        later_len.append(message(way, nat_part(C, way, 4, True, 1), nat_part(C, way, 4, False, 1)))
        later_len.append(message(way, nat_part(K, way, 3, True), nat_part(K, way, 3, False)))
    lax.fori_loop(1, 11, row_step, 0, unroll=5)
    lax.fori_loop(11, 31, row_step, 0, unroll=5)

    received(first_len)
    row(0)
    row(31)
    later_diag = []
    for way in diagonal:
        later_diag.append(message(way, strip_part(CT, way, 1, 3, True), strip_part(CT, way, 1, 3, False)))
        later_diag.append(message(way, strip_part(KT, way, 1, 2, True), strip_part(KT, way, 1, 2, False)))

    for side in range(2):
        for col in OWN_COLS[side]:
            if col not in (0, 31):
                for h in range(2):
                    E0T[side, col - FIRST[side], h, own_t, :] = column(E0, h, NAT0, col)
    second, second_len = [], []
    for way in wid_ways:
        second.append(message(way, strip_part(E0T, way, 2, 4, True), strip_part(E0T, way, 2, 4, False)))

    received(first_wid)
    for side, col, c, sign in edges:
        halo = c - 1 if side == 0 else c + 1
        for h in range(2):
            cond = QR[side, 1, h]
            CT[side, halo, h, own_t, :] = cond
            s = 0.5 * (CT[side, c, h, own_t, :] + cond)
            res = column(RP, h, 0, col) + s * (
                QR[side, 0, h] - sign * column(HW, h, PAD, col) - GT[side, c, h, own_t, :]
            )
            e = res / (column(DP, h, 0, col) + s)
            E0T[side, c, h, own_t, :] = e
            E0[h, pl.ds(NAT0 + col, 32, stride=32), :] = e
    for way in wid_ways:
        second.append(message(way, strip_part(E0T, way, 1, 1, True), strip_part(E0T, way, 1, 1, False)))
    for way in diagonal:
        second.append(message(way, strip_part(E0T, way, 1, 3, True), strip_part(E0T, way, 1, 3, False)))
    for way in len_ways:
        second_len.append(message(way, nat_part(E0, way, 4, True), nat_part(E0, way, 4, False)))
    for way in wid_ways:
        last.append(message(way, strip_part(GT, way, 1, 1, True), strip_part(GT, way, 1, 1, False)))
    for way in len_ways:
        into = 1 if way[0] < 0 else 0
        first = PAD if way[0] < 0 else PAD + 31 * 32
        second_len.append(message(way, G.at[:, pl.ds(first, 32), :], GH.at[into]))

    E = (E0, E1, E2)
    ET = (E0T, E1T, E2T, E3T)

    def sweep_row(k, r, guess=None):
        o = pl.multiple_of(32 * r, 32)
        src = E[k]
        x = [src[h, pl.ds(o, 32), :] for h in range(2)]
        xu, xd = k_up(x, False), k_down(x, False)
        for h in range(2):
            def t(q):
                return TN[q, h, pl.ds(o, 32), :]
            total = ALPHAS[k] * x[h] + t(4) * xd[h] + t(5) * xu[h]
            total = total + t(0) * src[h, pl.ds(o - 32, 32), :] + t(1) * src[h, pl.ds(o + 32, 32), :]
            total = total + t(2) * src[h, pl.ds(o - 1, 32), :] + t(3) * src[h, pl.ds(o + 1, 32), :]
            if k > 0:
                old = E[k - 1][h, pl.ds(o, 32), :]
                total = total + BETAS[k] * old
            if k < SWEEPS - 2:
                E[k + 1][h, pl.ds(o, 32), :] = total
            else:
                g = guess(h) if guess else G[h, pl.ds(pl.multiple_of(o - (NAT0 - PAD), 8), 32), :]
                pot = (g + GAINS[0] * E0[h, pl.ds(o, 32), :]) + GAINS[1] * old
                pot = (pot + GAINS[2] * x[h]) + GAINS[3] * total
                POT[h, pl.ds(pl.multiple_of(PW * r + 8, 8), 32), :] = pot

    def sweep(k, first, last, unroll):
        def step(r, carry):
            sweep_row(k, r)
            return carry
        lax.fori_loop(first + DEEP, last + 1 + DEEP, step, 0, unroll=unroll)

    sweep(0, 1, 30, 10)
    sweep(1, 2, 29, 14)
    sweep(2, 3, 28, 13)

    received(later_len)
    for i in (-3, -2, -1):
        row(i, has[-1, 0])
        row(31 - i, has[1, 0])
    received(second_len)
    for k in range(SWEEPS - 1):
        for i in (*range(k - 3, k + 1), *range(31 - k, 35 - k)):
            guess = None
            if i == -1:
                guess = lambda h: GH[0, h]
            if i == 32:
                guess = lambda h: GH[1, h]
            sweep_row(k, i + DEEP, guess)
    for side in range(2):
        for col in OWN_COLS[side]:
            c = col - FIRST[side]
            for h in range(2):
                E0T[side, c, h, pl.ds(12, 4), :] = column(E0, h, 0, col, 4)
                E0T[side, c, h, pl.ds(48, 4), :] = column(E0, h, NAT0 + 1024, col, 4)
                if 3 <= c <= 6:
                    GT[side, c, h, pl.ds(15, 1), :] = GH[0, h, pl.ds(col, 1), :]
                    GT[side, c, h, pl.ds(48, 1), :] = GH[1, h, pl.ds(col, 1), :]
                if col in (1, 2, 29, 30):
                    E1T[side, c, h, TAREA, :] = column(E1, h, 0, col, 40)
                if col in (2, 3, 28, 29):
                    E2T[side, c, h, TAREA, :] = column(E2, h, 0, col, 40)

    def finish(first, count, unroll):
        def step(i, carry):
            n = pl.multiple_of(32 * i + first, 8)
            q = pl.multiple_of(PW * (i + DEEP) + 8 + first, 8)
            for h in range(2):
                at = (h, pl.ds(n, count), slice(None))
                lanes = pl.ds(128 * h, 128)
                pot_out[pl.ds(n, count), lanes] = POT[h, pl.ds(q, count), :]
                vel_out[0, pl.ds(n, count), lanes] = U0[at] - B[at] * (
                    POT[h, pl.ds(q + 1, count), :] - POT[h, pl.ds(q - 1, count), :]
                )
                vel_out[1, pl.ds(n, count), lanes] = U1[at] + B[at] * (
                    POT[h, pl.ds(q + PW, count), :] - POT[h, pl.ds(q - PW, count), :]
                )
            return carry

        lax.fori_loop(0, 32, step, 0, unroll=unroll)

    finish(8, 16, 4)
    received(later_wid)
    received(later_diag)
    for side in range(2):
        for col in OWN_COLS[side]:
            c = col - FIRST[side]
            for h in range(2):
                CT[side, c, h, pl.ds(12, 4), :] = column(C, h, 0, col, 4)
                CT[side, c, h, pl.ds(48, 4), :] = column(C, h, NAT0 + 1024, col, 4)
                if 3 <= c <= 6:
                    KT[side, c, h, pl.ds(13, 3), :] = column(K, h, 32, col, 3)
                    KT[side, c, h, pl.ds(48, 3), :] = column(K, h, NAT0 + 1024, col, 3)


    ii = lax.broadcasted_iota(jnp.int32, (40, 128), 0)
    rows_in = jnp.logical_and(
        jnp.logical_or(ii >= 4, has[-1, 0]), jnp.logical_or(ii < 36, has[1, 0])
    )

    for side in range(2):
        has_side = has[0, -1 if side == 0 else 1]

        def strip(c, carry):
            x = [CT[side, c, h, TAREA, :] for h in range(2)]
            cu, cd = k_up(x, True), k_down(x, True)
            in_own = c >= 4 if side == 0 else c < 6
            valid = jnp.logical_and(rows_in, jnp.logical_or(in_own, has_side))
            for h in range(2):
                slm = 0.5 * (x[h] + CT[side, c, h, pl.ds(11, 40), :])
                slp = 0.5 * (x[h] + CT[side, c, h, pl.ds(13, 40), :])
                swm = 0.5 * (x[h] + CT[side, c - 1, h, TAREA, :])
                swp = 0.5 * (x[h] + CT[side, c + 1, h, TAREA, :])
                skm, skp = 0.5 * (x[h] + cd[h]), 0.5 * (x[h] + cu[h])
                diag = 2.0 * KT[side, c, h, TAREA, :] + ((slm + slp) + (swm + swp)) + (skm + skp)
                iv = jnp.where(valid, 1.0 / diag, 0.0)

                def store(q, t):
                    TT[q, side, c, h, TAREA, :] = t

                put_coefficients(iv, h, (slm, slp, swm, swp, skm, skp), store)
            return carry

        for c in range(1, 7) if side == 0 else range(3, 9):
            strip(c, 0)

    received(second)

    for k in range(SWEEPS - 1):
        for side in range(2):
            def strip_sweep(c, carry):
                src = ET[k]
                x = [src[side, c, h, TAREA, :] for h in range(2)]
                xu, xd = k_up(x, False), k_down(x, False)
                for h in range(2):
                    def t(q):
                        return TT[q, side, c, h, TAREA, :]
                    total = ALPHAS[k] * x[h] + t(4) * xd[h] + t(5) * xu[h]
                    total = total + t(0) * src[side, c, h, pl.ds(11, 40), :] + t(1) * src[side, c, h, pl.ds(13, 40), :]
                    total = total + t(2) * src[side, c - 1, h, TAREA, :] + t(3) * src[side, c + 1, h, TAREA, :]
                    if k > 0:
                        total = total + BETAS[k] * ET[k - 1][side, c, h, TAREA, :]
                    ET[k + 1][side, c, h, TAREA, :] = total
                return carry

            for c in range(1 + k, 5 + k) if side == 0 else range(5 - k, 9 - k):
                strip_sweep(c, 0)

    received(last)
    for side in range(2):
        for c in range(3, 7):
            for h in range(2):
                total = GT[side, c, h, TAREA, :]
                for k in range(SWEEPS):
                    total = total + GAINS[k] * ET[k][side, c, h, TAREA, :]
                POT[h, pl.ds(8 + c + FIRST[side], 40, stride=PW), :] = total
    finish(0, 8, 4)
    finish(24, 8, 4)

    for way, copy in sent:
        @pl.when(has[way])
        def _():
            copy.wait_send()


N_MESSAGES = 36


def deliver(vel, pot, vel_out, pot_out, sem):
    copies = []
    for half in range(2):
        rows = pl.ds(512 * half, 512)
        for src, dst in ((vel.at[0, rows], vel_out.at[0, rows]), (vel.at[1, rows], vel_out.at[1, rows]), (pot.at[rows], pot_out.at[rows])):
            copies.append(pltpu.make_async_copy(src, dst, sem.at[len(copies)]))
    for copy in copies:
        copy.start()
    for copy in copies:
        copy.wait()


def solution(mesh):
    n_len, n_wid = mesh.shape["len"], mesh.shape["wid"]

    def body(velocity, bfield, material, wall_mask, potential_guess):
        flat = lambda a: pltpu.with_memory_space_constraint(a.reshape(a.shape[:-3] + (1024, 256)), pltpu.HBM)
        own = pltpu.VMEM((2, 1024, 128), jnp.float32)
        padded = pltpu.VMEM((2, 1024 + 2 * PAD, 128), jnp.float32)
        nat = pltpu.VMEM((2, 1024 + 2 * NAT0, 128), jnp.float32)
        strip = pltpu.VMEM((2, 10, 2, TROWS, 128), jnp.float32)
        ints = pltpu.VMEM((2, 1024, 128), jnp.int32)
        rows = pltpu.VMEM((2, 2, 32, 128), jnp.float32)
        crit = pltpu.VMEM((2, 2, 2, 32, 128), jnp.float32)
        scratch = [
            own, own, own, ints, ints, padded, own, padded, nat, nat, nat, nat, own, own, nat, nat, nat,
            pltpu.VMEM((6, 2, 1024 + 2 * NAT0, 128), jnp.float32), rows,
            strip, strip, strip, crit, crit, strip, strip, strip, strip,
            pltpu.VMEM((6, 2, 10, 2, TROWS, 128), jnp.float32),
            pltpu.VMEM((2, 40 * PW, 128), jnp.float32),
            pltpu.SemaphoreType.DMA((12,)),
            pltpu.SemaphoreType.DMA((N_MESSAGES,)),
            pltpu.SemaphoreType.DMA((N_MESSAGES,)),
        ]
        vel, pot = pl.pallas_call(
            functools.partial(kernel, n_len, n_wid),
            out_shape=(
                pltpu.VMEM((2, 1024, 256), jnp.float32),
                pltpu.VMEM((1024, 256), jnp.float32),
            ),
            in_specs=[pl.BlockSpec(memory_space=pltpu.HBM)] * 5,
            out_specs=(pl.BlockSpec(memory_space=pltpu.VMEM), pl.BlockSpec(memory_space=pltpu.VMEM)),
            scratch_shapes=scratch,
            compiler_params=pltpu.CompilerParams(
                collective_id=0, has_side_effects=True, vmem_limit_bytes=50 * 1024 * 1024
            ),
        )(flat(velocity), flat(bfield), flat(material), flat(wall_mask), flat(potential_guess))
        vel, pot = pl.pallas_call(
            deliver,
            out_shape=(
                jax.ShapeDtypeStruct((2, 1024, 256), jnp.float32),
                jax.ShapeDtypeStruct((1024, 256), jnp.float32),
            ),
            in_specs=[pl.BlockSpec(memory_space=pltpu.VMEM)] * 2,
            out_specs=(pl.BlockSpec(memory_space=pltpu.HBM), pl.BlockSpec(memory_space=pltpu.HBM)),
            scratch_shapes=[pltpu.SemaphoreType.DMA((6,))],
        )(*(pltpu.with_memory_space_constraint(a, pltpu.VMEM) for a in (vel, pot)))
        return vel.reshape(velocity.shape), pot.reshape(bfield.shape)

    whole, part = P(None, "len", "wid", None), P("len", "wid", None)
    return jax.shard_map(
        body,
        mesh=mesh,
        in_specs=(whole, part, part, part, part),
        out_specs=(whole, part),
        check_vma=False,
    )
```

```python
import functools

import jax
import jax.numpy as jnp
from jax import lax
from jax.experimental import pallas as pl
from jax.experimental.pallas import tpu as pltpu
from jax.sharding import PartitionSpec as P

MESH = pl.DeviceIdType.MESH
SWEEPS = 4
THETA = 0.5 * (2.0 + 0.1)
DELTA = 0.5 * (2.0 - 0.1)
S1 = THETA / DELTA

ROWS = 32
DEEP = 4
NAT0 = DEEP * 32
PAD = 8
TROWS = 64
TOWN = 16
TAREA = pl.ds(12, 40)
PW = 48
FIRST = (-4, 26)
OWN_COLS = (range(0, 4), range(28, 32))


def chebyshev():
    weight = 1.0 / S1
    gains, alphas, betas = [1.0 / THETA], [], []
    kf_old = nf_old = None
    for _ in range(SWEEPS - 1):
        weight_next = 1.0 / (2.0 * S1 - weight)
        kf, nf = weight_next * weight, 2.0 * weight_next / DELTA
        if nf_old is None:
            alphas.append(kf / nf + THETA - 1.0)
            betas.append(0.0)
        else:
            alphas.append(kf / nf + 1.0 / nf_old - 1.0)
            betas.append(-kf_old / (nf_old * nf_old))
        gains.append(nf * gains[-1])
        kf_old, nf_old, weight = kf, nf, weight_next
    return gains, alphas, betas


GAINS, ALPHAS, BETAS = chebyshev()


def lanes_of(shape):
    return lax.broadcasted_iota(jnp.int32, shape, 1)


def k_up(x, zero):
    r = [pltpu.roll(v, 127, 1) for v in x]
    last = lanes_of(x[0].shape) == 127
    return [jnp.where(last, r[1], r[0]), jnp.where(last, 0.0, r[1]) if zero else r[1]]


def k_down(x, zero):
    r = [pltpu.roll(v, 1, 1) for v in x]
    first = lanes_of(x[0].shape) == 0
    return [jnp.where(first, 0.0, r[0]) if zero else r[0], jnp.where(first, r[0], r[1])]


def results(U0, U1, B, POT, h, i, first, count):
    n = pl.multiple_of(32 * i + first, 8)
    q = pl.multiple_of(PW * (i + DEEP) + 8 + first, 8)
    at = (h, pl.ds(n, count), slice(None))
    new_len = U0[at] - B[at] * (POT[h, pl.ds(q + 1, count), :] - POT[h, pl.ds(q - 1, count), :])
    new_wid = U1[at] + B[at] * (POT[h, pl.ds(q + PW, count), :] - POT[h, pl.ds(q - PW, count), :])
    return new_len, new_wid, POT[h, pl.ds(q, count), :]


def kernel(n_len, n_wid, u_hbm, b_hbm, m_hbm, w_hbm, g_hbm, vel_out, pot_out, U0, U1, B, POT,
           MAT, WALL, G, HL, HW, QP, QM, C, K, RP, DP, E0, E1, E2, TN, GH,
           CT, KT, GT, QS, QR, E0T, E1T, E2T, E3T, TT, lsem, ssem, rsem):
    li, wi = lax.axis_index("len"), lax.axis_index("wid")
    has = {(-1, 0): li > 0, (1, 0): li < n_len - 1, (0, -1): wi > 0, (0, 1): wi < n_wid - 1}
    for dl in (-1, 1):
        for dw in (-1, 1):
            has[dl, dw] = jnp.logical_and(has[dl, 0], has[0, dw])
    straight = ((0, -1), (0, 1), (-1, 0), (1, 0))
    diagonal = ((-1, -1), (-1, 1), (1, -1), (1, 1))

    barrier = pltpu.get_barrier_semaphore()
    for way in straight:
        @pl.when(has[way])
        def _():
            pl.semaphore_signal(barrier, inc=1, device_id=(li + way[0], wi + way[1]), device_id_type=MESH)

    own = pl.ds(PAD, 1024)
    loads = []
    for src, dst in (
        (m_hbm, lambda h: MAT.at[h]), (u_hbm.at[0], lambda h: U0.at[h]), (b_hbm, lambda h: B.at[h]),
        (g_hbm, lambda h: G.at[h, own]), (u_hbm.at[1], lambda h: U1.at[h]), (w_hbm, lambda h: WALL.at[h]),
    ):
        for h in range(2):
            copy = pltpu.make_async_copy(src.at[:, pl.ds(128 * h, 128)], dst(h), lsem.at[len(loads)])
            copy.start()
            loads.append(copy)

    for dl in (-1, 1):
        rows = pl.ds(0, 128) if dl < 0 else pl.ds(NAT0 + 1024, 128)
        @pl.when(jnp.logical_not(has[dl, 0]))
        def _():
            for ref in (C, K, E0, QP, QM):
                for h in range(2):
                    ref[h, rows, :] = jnp.zeros((128, 128), jnp.float32)
            for h in range(2):
                GH[(dl + 1) // 2, h] = jnp.zeros((32, 128), jnp.float32)
    for dw in (-1, 1):
        side = (dw + 1) // 2
        c0 = 0 if dw < 0 else 6
        @pl.when(jnp.logical_not(has[0, dw]))
        def _():
            for h in range(2):
                for kind in range(2):
                    QR[side, kind, h] = jnp.zeros((32, 128), jnp.float32)
                for c in range(c0, c0 + 4):
                    for ref in (CT, KT, GT, E0T):
                        ref[side, c, h, pl.ds(TOWN, 32), :] = jnp.zeros((32, 128), jnp.float32)
    for dl, dw in diagonal:
        side = (dw + 1) // 2
        c0 = 0 if dw < 0 else 6
        @pl.when(jnp.logical_not(has[dl, dw]))
        def _():
            for h in range(2):
                for c in range(c0, c0 + 4):
                    for ref in (CT, KT, E0T):
                        ref[side, c, h, pl.ds(8 if dl < 0 else 48, 8), :] = jnp.zeros((8, 128), jnp.float32)

    def column(ref, h, first, col, rows=32):
        return ref[h, pl.ds(first + col, rows, stride=32), :]

    def conduct(m):
        return jnp.where(m == 0, 1.0, jnp.where(m == 1, 0.5, 6.0))

    own_t = pl.ds(TOWN, 32)
    edges = ((0, 0, 4, -1.0), (1, 31, 5, 1.0))
    for copy in loads[:8]:
        copy.wait()
    for side, col, c, sign in edges:
        for h in range(2):
            g = column(G, h, PAD, col)
            cond = conduct(column(MAT, h, 0, col))
            CT[side, c, h, own_t, :] = cond
            GT[side, c, h, own_t, :] = g
            QS[side, 1, h] = cond
            QS[side, 0, h] = g - sign * (0.5 * (column(U0, h, 0, col) * column(B, h, 0, col)))
    for copy in loads[8:]:
        copy.wait()

    def prepare(i, carry):
        n = pl.multiple_of(32 * i, 32)
        o, p = pl.multiple_of(NAT0 + n, 32), pl.multiple_of(PAD + n, 8)
        for h in range(2):
            m = MAT[h, pl.ds(n, 32), :]
            b, g = B[h, pl.ds(n, 32), :], G[h, pl.ds(p, 32), :]
            hl = 0.5 * (U1[h, pl.ds(n, 32), :] * b)
            C[h, pl.ds(o, 32), :] = conduct(m)
            K[h, pl.ds(o, 32), :] = WALL[h, pl.ds(n, 32), :].astype(jnp.float32)
            HL[h, pl.ds(n, 32), :] = hl
            HW[h, pl.ds(p, 32), :] = -0.5 * (U0[h, pl.ds(n, 32), :] * b)
            QP[h, pl.ds(o, 32), :] = g + hl
            QM[h, pl.ds(o, 32), :] = g - hl
        return carry

    lax.fori_loop(0, 32, prepare, 0, unroll=4)

    sent = []

    def message(way, src, dst):
        k = len(sent)
        copy = pltpu.make_async_remote_copy(
            src, dst, ssem.at[k], rsem.at[k], device_id=(li + way[0], wi + way[1]), device_id_type=MESH
        )
        sent.append((way, copy))
        @pl.when(has[way])
        def _():
            copy.start()
        return way, copy

    def received(messages):
        for way, copy in messages:
            @pl.when(has[-way[0], -way[1]])
            def _():
                copy.wait_recv()

    def nat_part(ref, way, depth, here, skip=0):
        if way[0] < 0:
            first = (NAT0 if here else NAT0 + 1024) + 32 * skip
        else:
            first = NAT0 + 1024 - 32 * depth if here else NAT0 - 32 * depth
        return ref.at[:, pl.ds(first, 32 * (depth - skip)), :]

    def strip_part(ref, way, near, far, here):
        count = far - near + 1
        if way[1] < 0:
            side, first = (0, 3 + near) if here else (1, 5 + near)
        else:
            side, first = (1, 6 - far) if here else (0, 4 - far)
        if way[0] == 0:
            rows = own_t
        elif way[0] < 0:
            rows = pl.ds(16 if here else 48, far)
        else:
            rows = pl.ds((48 if here else 16) - far, far)
        return ref.at[side, pl.ds(first, count), :, rows, :]

    pl.semaphore_wait(barrier, sum(has[way].astype(jnp.int32) for way in straight))

    wid_ways, len_ways = straight[:2], straight[2:]
    first_wid, first_len, later_len, later_wid, last = [], [], [], [], []
    for way in wid_ways:
        out, into = (0, 1) if way[1] < 0 else (1, 0)
        first_wid.append(message(way, QS.at[out], QR.at[into]))
    for way in len_ways:
        Q = QM if way[0] < 0 else QP
        first_len.append(message(way, nat_part(Q, way, 1, True), nat_part(Q, way, 1, False)))
        first_len.append(message(way, nat_part(C, way, 1, True), nat_part(C, way, 1, False)))
    for side in range(2):
        for col in OWN_COLS[side]:
            c = col - FIRST[side]
            for h in range(2):
                if col not in (0, 31):
                    CT[side, c, h, own_t, :] = column(C, h, NAT0, col)
                    if 3 <= c <= 6:
                        GT[side, c, h, own_t, :] = column(G, h, PAD, col)
                KT[side, c, h, own_t, :] = column(K, h, NAT0, col)

    shape = (32, 128)
    jj = lax.broadcasted_iota(jnp.int32, shape, 0)
    lane = lanes_of(shape)

    def put_coefficients(iv, h, s, store):
        for q in range(6):
            t = s[q] * iv
            if q == 4 and h == 0:
                t = jnp.where(lanes_of(t.shape) == 0, 0.0, t)
            if q == 5 and h == 1:
                t = jnp.where(lanes_of(t.shape) == 127, 0.0, t)
            store(q, t)

    def row(i, valid=None):
        n = pl.multiple_of(32 * i, 32)
        o = pl.multiple_of(NAT0 + n, 32)
        p = pl.multiple_of(PAD + n, 8)
        c = [C[h, pl.ds(o, 32), :] for h in range(2)]
        cu, cd = k_up(c, True), k_down(c, True)
        if valid is None:
            g = [G[h, pl.ds(p, 32), :] for h in range(2)]
            gu, gd = k_up(g, True), k_down(g, True)
        for h in range(2):
            slm = 0.5 * (c[h] + C[h, pl.ds(o - 32, 32), :])
            slp = 0.5 * (c[h] + C[h, pl.ds(o + 32, 32), :])
            swm = jnp.where(jj == 0, 0.0, 0.5 * (c[h] + C[h, pl.ds(o - 1, 32), :]))
            swp = jnp.where(jj == 31, 0.0, 0.5 * (c[h] + C[h, pl.ds(o + 1, 32), :]))
            skm, skp = 0.5 * (c[h] + cd[h]), 0.5 * (c[h] + cu[h])
            k2 = 2.0 * K[h, pl.ds(o, 32), :]
            diag = k2 + ((slm + slp) + (swm + swp)) + (skm + skp)
            iv = 1.0 / diag
            if valid is None:
                hl, hw = HL[h, pl.ds(n, 32), :], HW[h, pl.ds(p, 32), :]
                gwm = jnp.where(jj == 0, 0.0, G[h, pl.ds(p - 1, 32), :] + HW[h, pl.ds(p - 1, 32), :] + hw)
                gwp = jnp.where(jj == 31, 0.0, G[h, pl.ds(p + 1, 32), :] - HW[h, pl.ds(p + 1, 32), :] - hw)
                res = slm * (QP[h, pl.ds(o - 32, 32), :] + hl) + slp * (QM[h, pl.ds(o + 32, 32), :] - hl)
                res = res + (swm * gwm + swp * gwp) + (skm * gd[h] + skp * gu[h]) - diag * g[h]
                at = (h, pl.ds(n, 32), slice(None))
                cb = c[h] * B[at]
                U0[at] = U0[at] + cb * hw
                U1[at] = U1[at] - cb * hl
                B[at] = 0.25 * cb
                RP[h, pl.ds(n, 32), :] = res
                DP[h, pl.ds(n, 32), :] = diag
                E0[h, pl.ds(o, 32), :] = res * iv
            else:
                iv = jnp.where(valid, iv, 0.0)

            def store(q, t):
                TN[q, h, pl.ds(o, 32), :] = t

            put_coefficients(iv, h, (slm, slp, swm, swp, skm, skp), store)

    def row_step(i, carry):
        row(i)
        return carry

    for way in wid_ways:
        later_wid.append(message(way, strip_part(CT, way, 2, 4, True), strip_part(CT, way, 2, 4, False)))
        later_wid.append(message(way, strip_part(KT, way, 1, 3, True), strip_part(KT, way, 1, 3, False)))
    for way in len_ways:
        later_len.append(message(way, nat_part(C, way, 4, True, 1), nat_part(C, way, 4, False, 1)))
        later_len.append(message(way, nat_part(K, way, 3, True), nat_part(K, way, 3, False)))
    lax.fori_loop(1, 11, row_step, 0, unroll=5)
    lax.fori_loop(11, 31, row_step, 0, unroll=5)

    received(first_len)
    row(0)
    row(31)
    later_diag = []
    for way in diagonal:
        later_diag.append(message(way, strip_part(CT, way, 1, 3, True), strip_part(CT, way, 1, 3, False)))
        later_diag.append(message(way, strip_part(KT, way, 1, 2, True), strip_part(KT, way, 1, 2, False)))

    for side in range(2):
        for col in OWN_COLS[side]:
            if col not in (0, 31):
                for h in range(2):
                    E0T[side, col - FIRST[side], h, own_t, :] = column(E0, h, NAT0, col)
    second, second_len = [], []
    for way in wid_ways:
        second.append(message(way, strip_part(E0T, way, 2, 4, True), strip_part(E0T, way, 2, 4, False)))

    received(first_wid)
    for side, col, c, sign in edges:
        halo = c - 1 if side == 0 else c + 1
        for h in range(2):
            cond = QR[side, 1, h]
            CT[side, halo, h, own_t, :] = cond
            s = 0.5 * (CT[side, c, h, own_t, :] + cond)
            res = column(RP, h, 0, col) + s * (
                QR[side, 0, h] - sign * column(HW, h, PAD, col) - GT[side, c, h, own_t, :]
            )
            e = res / (column(DP, h, 0, col) + s)
            E0T[side, c, h, own_t, :] = e
            E0[h, pl.ds(NAT0 + col, 32, stride=32), :] = e
    for way in wid_ways:
        second.append(message(way, strip_part(E0T, way, 1, 1, True), strip_part(E0T, way, 1, 1, False)))
    for way in diagonal:
        second.append(message(way, strip_part(E0T, way, 1, 3, True), strip_part(E0T, way, 1, 3, False)))
    for way in len_ways:
        second_len.append(message(way, nat_part(E0, way, 4, True), nat_part(E0, way, 4, False)))
    for way in wid_ways:
        last.append(message(way, strip_part(GT, way, 1, 1, True), strip_part(GT, way, 1, 1, False)))
    for way in len_ways:
        into = 1 if way[0] < 0 else 0
        first = PAD if way[0] < 0 else PAD + 31 * 32
        second_len.append(message(way, G.at[:, pl.ds(first, 32), :], GH.at[into]))

    E = (E0, E1, E2)
    ET = (E0T, E1T, E2T, E3T)

    def sweep_row(k, r, guess=None):
        o = pl.multiple_of(32 * r, 32)
        src = E[k]
        x = [src[h, pl.ds(o, 32), :] for h in range(2)]
        xu, xd = k_up(x, False), k_down(x, False)
        for h in range(2):
            def t(q):
                return TN[q, h, pl.ds(o, 32), :]
            total = ALPHAS[k] * x[h] + t(4) * xd[h] + t(5) * xu[h]
            total = total + t(0) * src[h, pl.ds(o - 32, 32), :] + t(1) * src[h, pl.ds(o + 32, 32), :]
            total = total + t(2) * src[h, pl.ds(o - 1, 32), :] + t(3) * src[h, pl.ds(o + 1, 32), :]
            if k > 0:
                old = E[k - 1][h, pl.ds(o, 32), :]
                total = total + BETAS[k] * old
            if k < SWEEPS - 2:
                E[k + 1][h, pl.ds(o, 32), :] = total
            else:
                g = guess(h) if guess else G[h, pl.ds(pl.multiple_of(o - (NAT0 - PAD), 8), 32), :]
                pot = (g + GAINS[0] * E0[h, pl.ds(o, 32), :]) + GAINS[1] * old
                pot = (pot + GAINS[2] * x[h]) + GAINS[3] * total
                POT[h, pl.ds(pl.multiple_of(PW * r + 8, 8), 32), :] = pot

    def sweep(k, first, last, unroll):
        def step(r, carry):
            sweep_row(k, r)
            return carry
        lax.fori_loop(first + DEEP, last + 1 + DEEP, step, 0, unroll=unroll)

    sweep(0, 1, 30, 10)
    sweep(1, 2, 29, 14)
    sweep(2, 3, 28, 13)

    received(later_len)
    for i in (-3, -2, -1):
        row(i, has[-1, 0])
        row(31 - i, has[1, 0])
    received(second_len)
    for k in range(SWEEPS - 1):
        for i in (*range(k - 3, k + 1), *range(31 - k, 35 - k)):
            guess = None
            if i == -1:
                guess = lambda h: GH[0, h]
            if i == 32:
                guess = lambda h: GH[1, h]
            sweep_row(k, i + DEEP, guess)
    for side in range(2):
        for col in OWN_COLS[side]:
            c = col - FIRST[side]
            for h in range(2):
                E0T[side, c, h, pl.ds(12, 4), :] = column(E0, h, 0, col, 4)
                E0T[side, c, h, pl.ds(48, 4), :] = column(E0, h, NAT0 + 1024, col, 4)
                if 3 <= c <= 6:
                    GT[side, c, h, pl.ds(15, 1), :] = GH[0, h, pl.ds(col, 1), :]
                    GT[side, c, h, pl.ds(48, 1), :] = GH[1, h, pl.ds(col, 1), :]
                if col in (1, 2, 29, 30):
                    E1T[side, c, h, TAREA, :] = column(E1, h, 0, col, 40)
                if col in (2, 3, 28, 29):
                    E2T[side, c, h, TAREA, :] = column(E2, h, 0, col, 40)

    def middle(i, carry):
        n = pl.multiple_of(32 * i + 8, 8)
        for h in range(2):
            lanes = pl.ds(128 * h, 128)
            new_len, new_wid, potential = results(U0, U1, B, POT, h, i, 8, 16)
            vel_out[0, pl.ds(n, 16), lanes] = new_len
            vel_out[1, pl.ds(n, 16), lanes] = new_wid
            pot_out[pl.ds(n, 16), lanes] = potential
        return carry

    lax.fori_loop(0, 32, middle, 0, unroll=4)
    received(later_wid)
    received(later_diag)
    for side in range(2):
        for col in OWN_COLS[side]:
            c = col - FIRST[side]
            for h in range(2):
                CT[side, c, h, pl.ds(12, 4), :] = column(C, h, 0, col, 4)
                CT[side, c, h, pl.ds(48, 4), :] = column(C, h, NAT0 + 1024, col, 4)
                if 3 <= c <= 6:
                    KT[side, c, h, pl.ds(13, 3), :] = column(K, h, 32, col, 3)
                    KT[side, c, h, pl.ds(48, 3), :] = column(K, h, NAT0 + 1024, col, 3)


    ii = lax.broadcasted_iota(jnp.int32, (40, 128), 0)
    rows_in = jnp.logical_and(
        jnp.logical_or(ii >= 4, has[-1, 0]), jnp.logical_or(ii < 36, has[1, 0])
    )

    for side in range(2):
        has_side = has[0, -1 if side == 0 else 1]

        def strip(c, carry):
            x = [CT[side, c, h, TAREA, :] for h in range(2)]
            cu, cd = k_up(x, True), k_down(x, True)
            in_own = c >= 4 if side == 0 else c < 6
            valid = jnp.logical_and(rows_in, jnp.logical_or(in_own, has_side))
            for h in range(2):
                slm = 0.5 * (x[h] + CT[side, c, h, pl.ds(11, 40), :])
                slp = 0.5 * (x[h] + CT[side, c, h, pl.ds(13, 40), :])
                swm = 0.5 * (x[h] + CT[side, c - 1, h, TAREA, :])
                swp = 0.5 * (x[h] + CT[side, c + 1, h, TAREA, :])
                skm, skp = 0.5 * (x[h] + cd[h]), 0.5 * (x[h] + cu[h])
                diag = 2.0 * KT[side, c, h, TAREA, :] + ((slm + slp) + (swm + swp)) + (skm + skp)
                iv = jnp.where(valid, 1.0 / diag, 0.0)

                def store(q, t):
                    TT[q, side, c, h, TAREA, :] = t

                put_coefficients(iv, h, (slm, slp, swm, swp, skm, skp), store)
            return carry

        for c in range(1, 7) if side == 0 else range(3, 9):
            strip(c, 0)

    received(second)

    for k in range(SWEEPS - 1):
        for side in range(2):
            def strip_sweep(c, carry):
                src = ET[k]
                x = [src[side, c, h, TAREA, :] for h in range(2)]
                xu, xd = k_up(x, False), k_down(x, False)
                for h in range(2):
                    def t(q):
                        return TT[q, side, c, h, TAREA, :]
                    total = ALPHAS[k] * x[h] + t(4) * xd[h] + t(5) * xu[h]
                    total = total + t(0) * src[side, c, h, pl.ds(11, 40), :] + t(1) * src[side, c, h, pl.ds(13, 40), :]
                    total = total + t(2) * src[side, c - 1, h, TAREA, :] + t(3) * src[side, c + 1, h, TAREA, :]
                    if k > 0:
                        total = total + BETAS[k] * ET[k - 1][side, c, h, TAREA, :]
                    ET[k + 1][side, c, h, TAREA, :] = total
                return carry

            for c in range(1 + k, 5 + k) if side == 0 else range(5 - k, 9 - k):
                strip_sweep(c, 0)

    received(last)
    for side in range(2):
        for c in range(3, 7):
            for h in range(2):
                total = GT[side, c, h, TAREA, :]
                for k in range(SWEEPS):
                    total = total + GAINS[k] * ET[k][side, c, h, TAREA, :]
                POT[h, pl.ds(8 + c + FIRST[side], 40, stride=PW), :] = total

    for way, copy in sent:
        @pl.when(has[way])
        def _():
            copy.wait_send()


N_MESSAGES = 36


def deliver(vel, pot, U0, U1, B, POT, vel_out, pot_out, outer, sem):
    copies = []

    def out(src, dst):
        copies.append(pltpu.make_async_copy(src, dst, sem.at[len(copies)]))
        copies[-1].start()

    inner = pl.ds(8, 16)
    for part in range(2):
        out(vel.at[part, :, inner], vel_out.at[part, :, inner])
    out(pot.at[:, inner], pot_out.at[:, inner])
    for side in range(2):
        first = 24 * side

        def step(i, carry):
            for h in range(2):
                lanes = pl.ds(128 * h, 128)
                for part, value in enumerate(results(U0, U1, B, POT, h, i, first, 8)):
                    outer[side, part, i, :, lanes] = value
            return carry

        lax.fori_loop(0, 32, step, 0, unroll=8)
        for part in range(2):
            out(outer.at[side, part], vel_out.at[part, :, pl.ds(first, 8)])
        out(outer.at[side, 2], pot_out.at[:, pl.ds(first, 8)])
    for copy in copies:
        copy.wait()


def solution(mesh):
    n_len, n_wid = mesh.shape["len"], mesh.shape["wid"]

    def body(velocity, bfield, material, wall_mask, potential_guess):
        flat = lambda a: pltpu.with_memory_space_constraint(a.reshape(a.shape[:-3] + (1024, 256)), pltpu.HBM)
        own = pltpu.VMEM((2, 1024, 128), jnp.float32)
        padded = pltpu.VMEM((2, 1024 + 2 * PAD, 128), jnp.float32)
        nat = pltpu.VMEM((2, 1024 + 2 * NAT0, 128), jnp.float32)
        strip = pltpu.VMEM((2, 10, 2, TROWS, 128), jnp.float32)
        ints = pltpu.VMEM((2, 1024, 128), jnp.int32)
        rows = pltpu.VMEM((2, 2, 32, 128), jnp.float32)
        crit = pltpu.VMEM((2, 2, 2, 32, 128), jnp.float32)
        scratch = [
            ints, ints, padded, own, padded, nat, nat, nat, nat, own, own, nat, nat, nat,
            pltpu.VMEM((6, 2, 1024 + 2 * NAT0, 128), jnp.float32), rows,
            strip, strip, strip, crit, crit, strip, strip, strip, strip,
            pltpu.VMEM((6, 2, 10, 2, TROWS, 128), jnp.float32),
            pltpu.SemaphoreType.DMA((12,)),
            pltpu.SemaphoreType.DMA((N_MESSAGES,)),
            pltpu.SemaphoreType.DMA((N_MESSAGES,)),
        ]
        kept = pl.pallas_call(
            functools.partial(kernel, n_len, n_wid),
            out_shape=(
                pltpu.VMEM((2, 1024, 256), jnp.float32),
                pltpu.VMEM((1024, 256), jnp.float32),
                own,
                own,
                own,
                pltpu.VMEM((2, 40 * PW, 128), jnp.float32),
            ),
            in_specs=[pl.BlockSpec(memory_space=pltpu.HBM)] * 5,
            out_specs=(pl.BlockSpec(memory_space=pltpu.VMEM),) * 6,
            scratch_shapes=scratch,
            compiler_params=pltpu.CompilerParams(
                collective_id=0, has_side_effects=True, vmem_limit_bytes=45 * 1024 * 1024
            ),
        )(flat(velocity), flat(bfield), flat(material), flat(wall_mask), flat(potential_guess))
        kept = (kept[0].reshape(2, 32, 32, 256), kept[1].reshape(32, 32, 256)) + tuple(kept[2:])
        return pl.pallas_call(
            deliver,
            out_shape=(
                jax.ShapeDtypeStruct((2, 32, 32, 256), jnp.float32),
                jax.ShapeDtypeStruct((32, 32, 256), jnp.float32),
            ),
            in_specs=[pl.BlockSpec(memory_space=pltpu.VMEM)] * 6,
            out_specs=(pl.BlockSpec(memory_space=pltpu.HBM), pl.BlockSpec(memory_space=pltpu.HBM)),
            scratch_shapes=[pltpu.VMEM((2, 3, 32, 8, 256), jnp.float32), pltpu.SemaphoreType.DMA((9,))],
            compiler_params=pltpu.CompilerParams(vmem_limit_bytes=8 * 1024 * 1024),
        )(*(pltpu.with_memory_space_constraint(a, pltpu.VMEM) for a in kept))

    whole, part = P(None, "len", "wid", None), P("len", "wid", None)
    return jax.shard_map(
        body,
        mesh=mesh,
        in_specs=(whole, part, part, part, part),
        out_specs=(whole, part),
        check_vma=False,
    )
```

```python
import functools

import jax
import jax.numpy as jnp
from jax import lax
from jax.experimental import pallas as pl
from jax.experimental.pallas import tpu as pltpu
from jax.sharding import PartitionSpec as P

MESH = pl.DeviceIdType.MESH
SWEEPS = 4
THETA = 0.5 * (2.0 + 0.1)
DELTA = 0.5 * (2.0 - 0.1)
S1 = THETA / DELTA

ROWS = 32
DEEP = 4
NAT0 = DEEP * 32
PAD = 8
TROWS = 64
TOWN = 16
TAREA = pl.ds(12, 40)
PW = 48
FIRST = (-4, 26)
OWN_COLS = (range(0, 4), range(28, 32))


def chebyshev():
    weight = 1.0 / S1
    gains, alphas, betas = [1.0 / THETA], [], []
    kf_old = nf_old = None
    for _ in range(SWEEPS - 1):
        weight_next = 1.0 / (2.0 * S1 - weight)
        kf, nf = weight_next * weight, 2.0 * weight_next / DELTA
        if nf_old is None:
            alphas.append(kf / nf + THETA - 1.0)
            betas.append(0.0)
        else:
            alphas.append(kf / nf + 1.0 / nf_old - 1.0)
            betas.append(-kf_old / (nf_old * nf_old))
        gains.append(nf * gains[-1])
        kf_old, nf_old, weight = kf, nf, weight_next
    return gains, alphas, betas


GAINS, ALPHAS, BETAS = chebyshev()


def lanes_of(shape):
    return lax.broadcasted_iota(jnp.int32, shape, 1)


def k_up(x, zero):
    r = [pltpu.roll(v, 127, 1) for v in x]
    last = lanes_of(x[0].shape) == 127
    return [jnp.where(last, r[1], r[0]), jnp.where(last, 0.0, r[1]) if zero else r[1]]


def k_down(x, zero):
    r = [pltpu.roll(v, 1, 1) for v in x]
    first = lanes_of(x[0].shape) == 0
    return [jnp.where(first, 0.0, r[0]) if zero else r[0], jnp.where(first, r[0], r[1])]


def results(U0, U1, B, POT, h, i, first, count):
    n = pl.multiple_of(32 * i + first, 8)
    q = pl.multiple_of(PW * (i + DEEP) + 8 + first, 8)
    at = (h, pl.ds(n, count), slice(None))
    new_len = U0[at] - B[at] * (POT[h, pl.ds(q + 1, count), :] - POT[h, pl.ds(q - 1, count), :])
    new_wid = U1[at] + B[at] * (POT[h, pl.ds(q + PW, count), :] - POT[h, pl.ds(q - PW, count), :])
    return new_len, new_wid, POT[h, pl.ds(q, count), :]


def kernel(n_len, n_wid, u_hbm, b_hbm, m_hbm, w_hbm, g_hbm, vel_out, pot_out, U0, U1, B, POT,
           MAT, WALL, G, HL, HW, QP, QM, C, K, RP, DP, E0, E1, E2, TN, GH,
           CT, KT, GT, QS, QR, E0T, E1T, E2T, E3T, TT, lsem, ssem, rsem):
    li, wi = lax.axis_index("len"), lax.axis_index("wid")
    has = {(-1, 0): li > 0, (1, 0): li < n_len - 1, (0, -1): wi > 0, (0, 1): wi < n_wid - 1}
    for dl in (-1, 1):
        for dw in (-1, 1):
            has[dl, dw] = jnp.logical_and(has[dl, 0], has[0, dw])
    straight = ((0, -1), (0, 1), (-1, 0), (1, 0))
    diagonal = ((-1, -1), (-1, 1), (1, -1), (1, 1))

    barrier = pltpu.get_barrier_semaphore()
    for way in straight:
        @pl.when(has[way])
        def _():
            pl.semaphore_signal(barrier, inc=1, device_id=(li + way[0], wi + way[1]), device_id_type=MESH)

    own = pl.ds(PAD, 1024)
    loads = []
    for src, dst in (
        (m_hbm, lambda h: MAT.at[h]), (u_hbm.at[0], lambda h: U0.at[h]), (b_hbm, lambda h: B.at[h]),
        (g_hbm, lambda h: G.at[h, own]), (u_hbm.at[1], lambda h: U1.at[h]), (w_hbm, lambda h: WALL.at[h]),
    ):
        for h in range(2):
            copy = pltpu.make_async_copy(src.at[:, pl.ds(128 * h, 128)], dst(h), lsem.at[len(loads)])
            copy.start()
            loads.append(copy)

    for dl in (-1, 1):
        rows = pl.ds(0, 128) if dl < 0 else pl.ds(NAT0 + 1024, 128)
        @pl.when(jnp.logical_not(has[dl, 0]))
        def _():
            for ref in (C, K, E0, QP, QM):
                for h in range(2):
                    ref[h, rows, :] = jnp.zeros((128, 128), jnp.float32)
            for h in range(2):
                GH[(dl + 1) // 2, h] = jnp.zeros((32, 128), jnp.float32)
    for dw in (-1, 1):
        side = (dw + 1) // 2
        c0 = 0 if dw < 0 else 6
        @pl.when(jnp.logical_not(has[0, dw]))
        def _():
            for h in range(2):
                for kind in range(2):
                    QR[side, kind, h] = jnp.zeros((32, 128), jnp.float32)
                for c in range(c0, c0 + 4):
                    for ref in (CT, KT, GT, E0T):
                        ref[side, c, h, pl.ds(TOWN, 32), :] = jnp.zeros((32, 128), jnp.float32)
    for dl, dw in diagonal:
        side = (dw + 1) // 2
        c0 = 0 if dw < 0 else 6
        @pl.when(jnp.logical_not(has[dl, dw]))
        def _():
            for h in range(2):
                for c in range(c0, c0 + 4):
                    for ref in (CT, KT, E0T):
                        ref[side, c, h, pl.ds(8 if dl < 0 else 48, 8), :] = jnp.zeros((8, 128), jnp.float32)

    def column(ref, h, first, col, rows=32):
        return ref[h, pl.ds(first + col, rows, stride=32), :]

    def conduct(m):
        return jnp.where(m == 0, 1.0, jnp.where(m == 1, 0.5, 6.0))

    own_t = pl.ds(TOWN, 32)
    edges = ((0, 0, 4, -1.0), (1, 31, 5, 1.0))
    for copy in loads[:8]:
        copy.wait()
    for side, col, c, sign in edges:
        for h in range(2):
            g = column(G, h, PAD, col)
            cond = conduct(column(MAT, h, 0, col))
            CT[side, c, h, own_t, :] = cond
            GT[side, c, h, own_t, :] = g
            QS[side, 1, h] = cond
            QS[side, 0, h] = g - sign * (0.5 * (column(U0, h, 0, col) * column(B, h, 0, col)))
    for copy in loads[8:]:
        copy.wait()

    def prepare(i, carry):
        n = pl.multiple_of(32 * i, 32)
        o, p = pl.multiple_of(NAT0 + n, 32), pl.multiple_of(PAD + n, 8)
        for h in range(2):
            m = MAT[h, pl.ds(n, 32), :]
            b, g = B[h, pl.ds(n, 32), :], G[h, pl.ds(p, 32), :]
            hl = 0.5 * (U1[h, pl.ds(n, 32), :] * b)
            C[h, pl.ds(o, 32), :] = conduct(m)
            K[h, pl.ds(o, 32), :] = WALL[h, pl.ds(n, 32), :].astype(jnp.float32)
            HL[h, pl.ds(n, 32), :] = hl
            HW[h, pl.ds(p, 32), :] = -0.5 * (U0[h, pl.ds(n, 32), :] * b)
            QP[h, pl.ds(o, 32), :] = g + hl
            QM[h, pl.ds(o, 32), :] = g - hl
        return carry

    prepare(0, 0)
    prepare(31, 0)

    sent = []

    def message(way, src, dst):
        k = len(sent)
        copy = pltpu.make_async_remote_copy(
            src, dst, ssem.at[k], rsem.at[k], device_id=(li + way[0], wi + way[1]), device_id_type=MESH
        )
        sent.append((way, copy))
        @pl.when(has[way])
        def _():
            copy.start()
        return way, copy

    def received(messages):
        for way, copy in messages:
            @pl.when(has[-way[0], -way[1]])
            def _():
                copy.wait_recv()

    def nat_part(ref, way, depth, here, skip=0):
        if way[0] < 0:
            first = (NAT0 if here else NAT0 + 1024) + 32 * skip
        else:
            first = NAT0 + 1024 - 32 * depth if here else NAT0 - 32 * depth
        return ref.at[:, pl.ds(first, 32 * (depth - skip)), :]

    def strip_part(ref, way, near, far, here):
        count = far - near + 1
        if way[1] < 0:
            side, first = (0, 3 + near) if here else (1, 5 + near)
        else:
            side, first = (1, 6 - far) if here else (0, 4 - far)
        if way[0] == 0:
            rows = own_t
        elif way[0] < 0:
            rows = pl.ds(16 if here else 48, far)
        else:
            rows = pl.ds((48 if here else 16) - far, far)
        return ref.at[side, pl.ds(first, count), :, rows, :]

    pl.semaphore_wait(barrier, sum(has[way].astype(jnp.int32) for way in straight))

    wid_ways, len_ways = straight[:2], straight[2:]
    first_wid, first_len, later_len, later_wid, last = [], [], [], [], []
    for way in wid_ways:
        out, into = (0, 1) if way[1] < 0 else (1, 0)
        first_wid.append(message(way, QS.at[out], QR.at[into]))
    for way in len_ways:
        Q = QM if way[0] < 0 else QP
        first_len.append(message(way, nat_part(Q, way, 1, True), nat_part(Q, way, 1, False)))
        first_len.append(message(way, nat_part(C, way, 1, True), nat_part(C, way, 1, False)))
    lax.fori_loop(1, 31, prepare, 0, unroll=5)
    for side in range(2):
        for col in OWN_COLS[side]:
            c = col - FIRST[side]
            for h in range(2):
                if col not in (0, 31):
                    CT[side, c, h, own_t, :] = column(C, h, NAT0, col)
                    if 3 <= c <= 6:
                        GT[side, c, h, own_t, :] = column(G, h, PAD, col)
                KT[side, c, h, own_t, :] = column(K, h, NAT0, col)

    shape = (32, 128)
    jj = lax.broadcasted_iota(jnp.int32, shape, 0)
    lane = lanes_of(shape)

    def put_coefficients(iv, h, s, store):
        for q in range(6):
            t = s[q] * iv
            if q == 4 and h == 0:
                t = jnp.where(lanes_of(t.shape) == 0, 0.0, t)
            if q == 5 and h == 1:
                t = jnp.where(lanes_of(t.shape) == 127, 0.0, t)
            store(q, t)

    def row(i, valid=None):
        n = pl.multiple_of(32 * i, 32)
        o = pl.multiple_of(NAT0 + n, 32)
        p = pl.multiple_of(PAD + n, 8)
        c = [C[h, pl.ds(o, 32), :] for h in range(2)]
        cu, cd = k_up(c, True), k_down(c, True)
        if valid is None:
            g = [G[h, pl.ds(p, 32), :] for h in range(2)]
            gu, gd = k_up(g, True), k_down(g, True)
        for h in range(2):
            slm = 0.5 * (c[h] + C[h, pl.ds(o - 32, 32), :])
            slp = 0.5 * (c[h] + C[h, pl.ds(o + 32, 32), :])
            swm = jnp.where(jj == 0, 0.0, 0.5 * (c[h] + C[h, pl.ds(o - 1, 32), :]))
            swp = jnp.where(jj == 31, 0.0, 0.5 * (c[h] + C[h, pl.ds(o + 1, 32), :]))
            skm, skp = 0.5 * (c[h] + cd[h]), 0.5 * (c[h] + cu[h])
            k2 = 2.0 * K[h, pl.ds(o, 32), :]
            diag = k2 + ((slm + slp) + (swm + swp)) + (skm + skp)
            iv = 1.0 / diag
            if valid is None:
                hl, hw = HL[h, pl.ds(n, 32), :], HW[h, pl.ds(p, 32), :]
                gwm = jnp.where(jj == 0, 0.0, G[h, pl.ds(p - 1, 32), :] + HW[h, pl.ds(p - 1, 32), :] + hw)
                gwp = jnp.where(jj == 31, 0.0, G[h, pl.ds(p + 1, 32), :] - HW[h, pl.ds(p + 1, 32), :] - hw)
                res = slm * (QP[h, pl.ds(o - 32, 32), :] + hl) + slp * (QM[h, pl.ds(o + 32, 32), :] - hl)
                res = res + (swm * gwm + swp * gwp) + (skm * gd[h] + skp * gu[h]) - diag * g[h]
                at = (h, pl.ds(n, 32), slice(None))
                cb = c[h] * B[at]
                U0[at] = U0[at] + cb * hw
                U1[at] = U1[at] - cb * hl
                B[at] = 0.25 * cb
                RP[h, pl.ds(n, 32), :] = res
                DP[h, pl.ds(n, 32), :] = diag
                E0[h, pl.ds(o, 32), :] = res * iv
            else:
                iv = jnp.where(valid, iv, 0.0)

            def store(q, t):
                TN[q, h, pl.ds(o, 32), :] = t

            put_coefficients(iv, h, (slm, slp, swm, swp, skm, skp), store)

    def row_step(i, carry):
        row(i)
        return carry

    for way in wid_ways:
        later_wid.append(message(way, strip_part(CT, way, 2, 4, True), strip_part(CT, way, 2, 4, False)))
        later_wid.append(message(way, strip_part(KT, way, 1, 3, True), strip_part(KT, way, 1, 3, False)))
    for way in len_ways:
        later_len.append(message(way, nat_part(C, way, 4, True, 1), nat_part(C, way, 4, False, 1)))
        later_len.append(message(way, nat_part(K, way, 3, True), nat_part(K, way, 3, False)))
    lax.fori_loop(1, 11, row_step, 0, unroll=5)
    lax.fori_loop(11, 31, row_step, 0, unroll=5)

    received(first_len)
    row(0)
    row(31)
    later_diag = []
    for way in diagonal:
        later_diag.append(message(way, strip_part(CT, way, 1, 3, True), strip_part(CT, way, 1, 3, False)))
        later_diag.append(message(way, strip_part(KT, way, 1, 2, True), strip_part(KT, way, 1, 2, False)))

    for side in range(2):
        for col in OWN_COLS[side]:
            if col not in (0, 31):
                for h in range(2):
                    E0T[side, col - FIRST[side], h, own_t, :] = column(E0, h, NAT0, col)
    second, second_len = [], []
    for way in wid_ways:
        second.append(message(way, strip_part(E0T, way, 2, 4, True), strip_part(E0T, way, 2, 4, False)))

    received(first_wid)
    for side, col, c, sign in edges:
        halo = c - 1 if side == 0 else c + 1
        for h in range(2):
            cond = QR[side, 1, h]
            CT[side, halo, h, own_t, :] = cond
            s = 0.5 * (CT[side, c, h, own_t, :] + cond)
            res = column(RP, h, 0, col) + s * (
                QR[side, 0, h] - sign * column(HW, h, PAD, col) - GT[side, c, h, own_t, :]
            )
            e = res / (column(DP, h, 0, col) + s)
            E0T[side, c, h, own_t, :] = e
            E0[h, pl.ds(NAT0 + col, 32, stride=32), :] = e
    for way in diagonal:
        second.append(message(way, strip_part(E0T, way, 1, 3, True), strip_part(E0T, way, 1, 3, False)))
    for way in wid_ways:
        second.append(message(way, strip_part(E0T, way, 1, 1, True), strip_part(E0T, way, 1, 1, False)))
    for way in len_ways:
        second_len.append(message(way, nat_part(E0, way, 4, True), nat_part(E0, way, 4, False)))
    for way in wid_ways:
        last.append(message(way, strip_part(GT, way, 1, 1, True), strip_part(GT, way, 1, 1, False)))
    for way in len_ways:
        into = 1 if way[0] < 0 else 0
        first = PAD if way[0] < 0 else PAD + 31 * 32
        second_len.append(message(way, G.at[:, pl.ds(first, 32), :], GH.at[into]))

    E = (E0, E1, E2)
    ET = (E0T, E1T, E2T, E3T)

    def sweep_row(k, r, guess=None):
        o = pl.multiple_of(32 * r, 32)
        src = E[k]
        x = [src[h, pl.ds(o, 32), :] for h in range(2)]
        xu, xd = k_up(x, False), k_down(x, False)
        for h in range(2):
            def t(q):
                return TN[q, h, pl.ds(o, 32), :]
            total = ALPHAS[k] * x[h] + t(4) * xd[h] + t(5) * xu[h]
            total = total + t(0) * src[h, pl.ds(o - 32, 32), :] + t(1) * src[h, pl.ds(o + 32, 32), :]
            total = total + t(2) * src[h, pl.ds(o - 1, 32), :] + t(3) * src[h, pl.ds(o + 1, 32), :]
            if k > 0:
                old = E[k - 1][h, pl.ds(o, 32), :]
                total = total + BETAS[k] * old
            if k < SWEEPS - 2:
                E[k + 1][h, pl.ds(o, 32), :] = total
            else:
                g = guess(h) if guess else G[h, pl.ds(pl.multiple_of(o - (NAT0 - PAD), 8), 32), :]
                pot = (g + GAINS[0] * E0[h, pl.ds(o, 32), :]) + GAINS[1] * old
                pot = (pot + GAINS[2] * x[h]) + GAINS[3] * total
                POT[h, pl.ds(pl.multiple_of(PW * r + 8, 8), 32), :] = pot

    def sweep(k, first, last, unroll):
        def step(r, carry):
            sweep_row(k, r)
            return carry
        lax.fori_loop(first + DEEP, last + 1 + DEEP, step, 0, unroll=unroll)

    sweep(0, 1, 30, 10)
    sweep(1, 2, 29, 14)
    sweep(2, 3, 28, 13)

    received(later_len)
    for i in (-3, -2, -1):
        row(i, has[-1, 0])
        row(31 - i, has[1, 0])
    received(second_len)
    for k in range(SWEEPS - 1):
        for i in (*range(k - 3, k + 1), *range(31 - k, 35 - k)):
            guess = None
            if i == -1:
                guess = lambda h: GH[0, h]
            if i == 32:
                guess = lambda h: GH[1, h]
            sweep_row(k, i + DEEP, guess)
    for side in range(2):
        for col in OWN_COLS[side]:
            c = col - FIRST[side]
            for h in range(2):
                E0T[side, c, h, pl.ds(12, 4), :] = column(E0, h, 0, col, 4)
                E0T[side, c, h, pl.ds(48, 4), :] = column(E0, h, NAT0 + 1024, col, 4)
                if 3 <= c <= 6:
                    GT[side, c, h, pl.ds(15, 1), :] = GH[0, h, pl.ds(col, 1), :]
                    GT[side, c, h, pl.ds(48, 1), :] = GH[1, h, pl.ds(col, 1), :]
                if col in (1, 2, 29, 30):
                    E1T[side, c, h, TAREA, :] = column(E1, h, 0, col, 40)
                if col in (2, 3, 28, 29):
                    E2T[side, c, h, TAREA, :] = column(E2, h, 0, col, 40)

    def middle(i, carry):
        n = pl.multiple_of(32 * i + 8, 8)
        for h in range(2):
            lanes = pl.ds(128 * h, 128)
            new_len, new_wid, potential = results(U0, U1, B, POT, h, i, 8, 16)
            vel_out[0, pl.ds(n, 16), lanes] = new_len
            vel_out[1, pl.ds(n, 16), lanes] = new_wid
            pot_out[pl.ds(n, 16), lanes] = potential
        return carry

    lax.fori_loop(0, 32, middle, 0, unroll=4)
    received(later_wid)
    received(later_diag)
    for side in range(2):
        for col in OWN_COLS[side]:
            c = col - FIRST[side]
            for h in range(2):
                CT[side, c, h, pl.ds(12, 4), :] = column(C, h, 0, col, 4)
                CT[side, c, h, pl.ds(48, 4), :] = column(C, h, NAT0 + 1024, col, 4)
                if 3 <= c <= 6:
                    KT[side, c, h, pl.ds(13, 3), :] = column(K, h, 32, col, 3)
                    KT[side, c, h, pl.ds(48, 3), :] = column(K, h, NAT0 + 1024, col, 3)


    ii = lax.broadcasted_iota(jnp.int32, (40, 128), 0)
    rows_in = jnp.logical_and(
        jnp.logical_or(ii >= 4, has[-1, 0]), jnp.logical_or(ii < 36, has[1, 0])
    )

    for side in range(2):
        has_side = has[0, -1 if side == 0 else 1]

        def strip(c, carry):
            x = [CT[side, c, h, TAREA, :] for h in range(2)]
            cu, cd = k_up(x, True), k_down(x, True)
            in_own = c >= 4 if side == 0 else c < 6
            valid = jnp.logical_and(rows_in, jnp.logical_or(in_own, has_side))
            for h in range(2):
                slm = 0.5 * (x[h] + CT[side, c, h, pl.ds(11, 40), :])
                slp = 0.5 * (x[h] + CT[side, c, h, pl.ds(13, 40), :])
                swm = 0.5 * (x[h] + CT[side, c - 1, h, TAREA, :])
                swp = 0.5 * (x[h] + CT[side, c + 1, h, TAREA, :])
                skm, skp = 0.5 * (x[h] + cd[h]), 0.5 * (x[h] + cu[h])
                diag = 2.0 * KT[side, c, h, TAREA, :] + ((slm + slp) + (swm + swp)) + (skm + skp)
                iv = jnp.where(valid, 1.0 / diag, 0.0)

                def store(q, t):
                    TT[q, side, c, h, TAREA, :] = t

                put_coefficients(iv, h, (slm, slp, swm, swp, skm, skp), store)
            return carry

        for c in range(1, 7) if side == 0 else range(3, 9):
            strip(c, 0)

    received(second)

    for k in range(SWEEPS - 1):
        for side in range(2):
            def strip_sweep(c, carry):
                src = ET[k]
                x = [src[side, c, h, TAREA, :] for h in range(2)]
                xu, xd = k_up(x, False), k_down(x, False)
                for h in range(2):
                    def t(q):
                        return TT[q, side, c, h, TAREA, :]
                    total = ALPHAS[k] * x[h] + t(4) * xd[h] + t(5) * xu[h]
                    total = total + t(0) * src[side, c, h, pl.ds(11, 40), :] + t(1) * src[side, c, h, pl.ds(13, 40), :]
                    total = total + t(2) * src[side, c - 1, h, TAREA, :] + t(3) * src[side, c + 1, h, TAREA, :]
                    if k > 0:
                        total = total + BETAS[k] * ET[k - 1][side, c, h, TAREA, :]
                    ET[k + 1][side, c, h, TAREA, :] = total
                return carry

            for c in range(1 + k, 5 + k) if side == 0 else range(5 - k, 9 - k):
                strip_sweep(c, 0)

    received(last)
    for side in range(2):
        for c in range(3, 7):
            for h in range(2):
                total = GT[side, c, h, TAREA, :]
                for k in range(SWEEPS):
                    total = total + GAINS[k] * ET[k][side, c, h, TAREA, :]
                POT[h, pl.ds(8 + c + FIRST[side], 40, stride=PW), :] = total

    for way, copy in sent:
        @pl.when(has[way])
        def _():
            copy.wait_send()


N_MESSAGES = 36


def deliver(vel, pot, U0, U1, B, POT, vel_out, pot_out, outer, sem):
    copies = []

    def out(src, dst):
        copies.append(pltpu.make_async_copy(src, dst, sem.at[len(copies)]))
        copies[-1].start()

    inner = pl.ds(8, 16)
    for part in range(2):
        out(vel.at[part, :, inner], vel_out.at[part, :, inner])
    out(pot.at[:, inner], pot_out.at[:, inner])
    for side in range(2):
        first = 24 * side

        def step(i, carry):
            for h in range(2):
                lanes = pl.ds(128 * h, 128)
                for part, value in enumerate(results(U0, U1, B, POT, h, i, first, 8)):
                    outer[side, part, i, :, lanes] = value
            return carry

        lax.fori_loop(0, 32, step, 0, unroll=8)
        for part in range(2):
            out(outer.at[side, part], vel_out.at[part, :, pl.ds(first, 8)])
        out(outer.at[side, 2], pot_out.at[:, pl.ds(first, 8)])
    for copy in copies:
        copy.wait()


def solution(mesh):
    n_len, n_wid = mesh.shape["len"], mesh.shape["wid"]

    def body(velocity, bfield, material, wall_mask, potential_guess):
        flat = lambda a: pltpu.with_memory_space_constraint(a.reshape(a.shape[:-3] + (1024, 256)), pltpu.HBM)
        own = pltpu.VMEM((2, 1024, 128), jnp.float32)
        padded = pltpu.VMEM((2, 1024 + 2 * PAD, 128), jnp.float32)
        nat = pltpu.VMEM((2, 1024 + 2 * NAT0, 128), jnp.float32)
        strip = pltpu.VMEM((2, 10, 2, TROWS, 128), jnp.float32)
        ints = pltpu.VMEM((2, 1024, 128), jnp.int32)
        rows = pltpu.VMEM((2, 2, 32, 128), jnp.float32)
        crit = pltpu.VMEM((2, 2, 2, 32, 128), jnp.float32)
        scratch = [
            ints, ints, padded, own, padded, nat, nat, nat, nat, own, own, nat, nat, nat,
            pltpu.VMEM((6, 2, 1024 + 2 * NAT0, 128), jnp.float32), rows,
            strip, strip, strip, crit, crit, strip, strip, strip, strip,
            pltpu.VMEM((6, 2, 10, 2, TROWS, 128), jnp.float32),
            pltpu.SemaphoreType.DMA((12,)),
            pltpu.SemaphoreType.DMA((N_MESSAGES,)),
            pltpu.SemaphoreType.DMA((N_MESSAGES,)),
        ]
        kept = pl.pallas_call(
            functools.partial(kernel, n_len, n_wid),
            out_shape=(
                pltpu.VMEM((2, 1024, 256), jnp.float32),
                pltpu.VMEM((1024, 256), jnp.float32),
                own,
                own,
                own,
                pltpu.VMEM((2, 40 * PW, 128), jnp.float32),
            ),
            in_specs=[pl.BlockSpec(memory_space=pltpu.HBM)] * 5,
            out_specs=(pl.BlockSpec(memory_space=pltpu.VMEM),) * 6,
            scratch_shapes=scratch,
            compiler_params=pltpu.CompilerParams(
                collective_id=0, has_side_effects=True, vmem_limit_bytes=45 * 1024 * 1024
            ),
        )(flat(velocity), flat(bfield), flat(material), flat(wall_mask), flat(potential_guess))
        kept = (kept[0].reshape(2, 32, 32, 256), kept[1].reshape(32, 32, 256)) + tuple(kept[2:])
        return pl.pallas_call(
            deliver,
            out_shape=(
                jax.ShapeDtypeStruct((2, 32, 32, 256), jnp.float32),
                jax.ShapeDtypeStruct((32, 32, 256), jnp.float32),
            ),
            in_specs=[pl.BlockSpec(memory_space=pltpu.VMEM)] * 6,
            out_specs=(pl.BlockSpec(memory_space=pltpu.HBM), pl.BlockSpec(memory_space=pltpu.HBM)),
            scratch_shapes=[pltpu.VMEM((2, 3, 32, 8, 256), jnp.float32), pltpu.SemaphoreType.DMA((9,))],
            compiler_params=pltpu.CompilerParams(vmem_limit_bytes=8 * 1024 * 1024),
        )(*(pltpu.with_memory_space_constraint(a, pltpu.VMEM) for a in kept))

    whole, part = P(None, "len", "wid", None), P("len", "wid", None)
    return jax.shard_map(
        body,
        mesh=mesh,
        in_specs=(whole, part, part, part, part),
        out_specs=(whole, part),
        check_vma=False,
    )
```
